256 devices in a mesh: blk: 16 (over y_lo, x, core), tm: 16 (over y_hi, z).
Axes of the slice: x: 4, y: 4 (y_hi: 2, y_lo: 2; y = y_hi * 2 + y_lo), z: 8, core: 2. Of those that a mesh axis runs over, the one named last changes fastest.
Arguments:
- rainfall: bfloat16 [10240, 8192], P('blk', 'tm'), as said below
- runoff: bfloat16 [10240, 8192], P('blk', 'tm'), as said below
- lag_days: int32 [1], replicated, may hold values from 0 to 30
Outputs:
- correlation: float32 [10240, 10240], P('blk', 'tm')
The draws below stay inside these ranges and needn't reach their ends.
Inputs may be any that keep to these rules, and one draw needn't show every extreme that they name: `rainfall`: every cell's precipitation and runoff anomalies both vary from day to day, so that both variances are positive. Every cell's runoff anomalies vary from day to day.
All inputs are finite; a program needn't handle non-finite values.
Results may differ from the reference program's by a relative error of at most 0.0003.
Values may be sent and summed in bfloat16 or wider, within the bound.
A program may use at most 128 MiB of HBM per device.

```python
import math
import jax
import jax.numpy as jnp
from jax import lax

EDGE = 32
CELLS = 10240
DAYS = 8192


def season_phases(key):
    return jax.random.uniform(key, (3,), jnp.float32, 0.0, 2.0 * math.pi)


def anomaly_field(key, phases, delay, jitter_scale, spread):
    first, second, third = jax.random.split(key, 3)
    loadings = jax.random.normal(first, (CELLS, 3), jnp.float32)
    offsets = jax.random.uniform(second, (CELLS, 1), jnp.float32, -1.0, 1.0)
    jitter = jax.random.normal(third, (CELLS, DAYS), jnp.float32)
    moments = jnp.arange(DAYS, dtype=jnp.float32) - delay
    field = offsets + jitter_scale * jitter
    for harmonic in range(3):
        seasonal = jnp.sin(2.0 * math.pi * (harmonic + 1) * moments / 365.0 + phases[harmonic] + spread * harmonic)
        field = field + loadings[:, harmonic:harmonic + 1] * seasonal[None, :]
    return field


def draw_rainfall(key, part):
    phases = season_phases(key)
    key = jax.random.fold_in(key, 11)
    return anomaly_field(key, phases, 0.0, 1.0, 0.0).astype(jnp.bfloat16)


def draw_runoff(key, part):
    phases = season_phases(key)
    key = jax.random.fold_in(key, 23)
    return anomaly_field(key, phases, 12.0, 0.8, 0.7).astype(jnp.bfloat16)


def setup_inputs(seed: int = 0) -> dict:
    arg_keys = jax.random.split(jax.random.key(seed), 4)
    return {
        "rainfall": draw_rainfall(jax.random.fold_in(arg_keys[3], 71), 0),
        "runoff": draw_runoff(jax.random.fold_in(arg_keys[3], 71), 0),
        "lag_days": jax.random.randint(arg_keys[2], (1,), 0, 31).astype(jnp.int32),
    }


def reference(rainfall, runoff, lag_days):
    shift_days = lag_days[0].astype(jnp.int32)
    total = rainfall.shape[1]
    padded = jnp.concatenate([runoff, jnp.zeros((runoff.shape[0], EDGE), runoff.dtype)], axis=1)
    moved = lax.dynamic_slice_in_dim(padded, shift_days, total, 1)
    valid = jnp.arange(total, dtype=jnp.int32) < total - shift_days
    rain_used = jnp.where(valid[None, :], rainfall, jnp.zeros_like(rainfall)).astype(jnp.float32)
    flow_used = jnp.where(valid[None, :], moved, jnp.zeros_like(moved)).astype(jnp.float32)
    samples = (total - shift_days).astype(jnp.float32)
    rain_sum = lax.optimization_barrier(jnp.sum(rain_used, axis=1))
    rain_square = lax.optimization_barrier(jnp.sum(rain_used * rain_used, axis=1))
    flow_sum = lax.optimization_barrier(jnp.sum(flow_used, axis=1))
    flow_square = lax.optimization_barrier(jnp.sum(flow_used * flow_used, axis=1))
    cross = jnp.dot(rain_used, flow_used.T, precision=lax.Precision.HIGHEST)
    covar = cross - rain_sum[:, None] * flow_sum[None, :] / samples
    rain_var = rain_square - rain_sum * rain_sum / samples
    flow_var = flow_square - flow_sum * flow_sum / samples
    return covar / jnp.sqrt(rain_var[:, None] * flow_var[None, :])
```

```python
import jax
import jax.numpy as jnp
from jax import lax
from jax.experimental import pallas as pl
from jax.experimental.pallas import tpu as pltpu
from jax.sharding import PartitionSpec as P

XS, ZS, LANES = 4, 8, 128
ORDER = (0, 1, 3, 2)
WAVES = ((0, 1), (2, 3))


def kernel(
    lag_ref, rain_ref, flow_ref, cross_ref, stat_ref,
    flow_v, rain_v, stage, rain_all, flow_all, acc, relay, final,
    rain_part, flow_part, stat_send, stat_recv,
    load_sem, s1, r1, s2, r2, s3, r3, sx, rx, sc, rc, sr, rr, se, re, sg, rg, sf, rf, st, rt,
):
    rows, days = rain_v.shape
    piece = rows // XS
    strip = rows // 4
    lag = lag_ref[0]
    blk, tm = lax.axis_index("blk"), lax.axis_index("tm")
    yl, x, c = lax.div(blk, 8), lax.rem(lax.div(blk, 2), 4), lax.rem(blk, 2)
    yh, z = lax.div(tm, 8), lax.rem(tm, 8)
    zp, zo = lax.div(z, 2), lax.rem(z, 2)
    other = 1 - yh

    def dev(yl_=None, x_=None, c_=None, yh_=None, z_=None):
        b = (yl if yl_ is None else yl_) * 8 + (x if x_ is None else x_) * 2 + (c if c_ is None else c_)
        t = (yh if yh_ is None else yh_) * 8 + (z if z_ is None else z_)
        return (b, t)

    def xo(d):
        return lax.rem(x + d, XS)

    def zo_(d):
        return lax.rem(z + d + ZS, ZS)

    y = 2 * yh + yl
    yu, yd = lax.rem(y + 1, 4), lax.rem(y + 3, 4)
    up = dev(yl_=lax.rem(yu, 2), yh_=lax.div(yu, 2))
    down = dev(yl_=lax.rem(yd, 2), yh_=lax.div(yd, 2))
    near = dev(yl_=1 - yl)
    sibling = dev(c_=1 - c)
    far = dev(yh_=other)
    far_sibling = dev(yh_=other, c_=1 - c)
    right, left = dev(x_=xo(1)), dev(x_=xo(3))
    ahead, behind = dev(z_=zo_(1)), dev(z_=zo_(-1))

    def swap_pair(k):
        return lax.rem(zp + k, 4)

    def swap_dev(k):
        return dev(z_=2 * swap_pair(k) + c, c_=zo)

    def rcopy(src, dst, send, recv, to):
        return pltpu.make_async_remote_copy(
            src_ref=src, dst_ref=dst, send_sem=send, recv_sem=recv,
            device_id=to, device_id_type=pl.DeviceIdType.MESH,
        )

    pending = []

    def send(copy, when=None):
        if when is None:
            copy.start()
        else:
            pl.when(when)(copy.start)
        pending.append((copy, when))

    load_flow = pltpu.make_async_copy(flow_ref, flow_v, load_sem.at[0])
    load_rain = pltpu.make_async_copy(rain_ref, rain_v, load_sem.at[1])
    load_flow.start()
    load_rain.start()

    crossed = c != zo
    barrier = pltpu.get_barrier_semaphore()
    partners = [dev(x_=xo(d)) for d in (1, 2, 3)]
    partners += [ahead, behind, up, down, far, far_sibling, sibling]
    partners += [swap_dev(k) for k in (1, 2, 3)]

    def greet(to):
        pl.semaphore_signal(barrier, inc=1, device_id=to, device_id_type=pl.DeviceIdType.MESH)

    for to in partners:
        greet(to)

    @pl.when(crossed)
    def _():
        greet(swap_dev(0))

    pl.semaphore_wait(barrier, len(partners) + jnp.where(crossed, 1, 0))

    def part(ref, i):
        return ref.at[pl.ds(pl.multiple_of(i * piece, piece), piece), :]

    def cell(zd, half, col):
        return flow_all.at[zd, half, pl.ds(pl.multiple_of(col * piece, piece), piece), :]

    load_flow.wait()
    own = pltpu.make_async_copy(part(flow_v, x), stage.at[0], r1.at[0])
    own.start()
    for d in (1, 3, 2):
        send(rcopy(part(flow_v, xo(d)), stage.at[d], s1.at[d], r1.at[d], dev(x_=xo(d))))

    load_rain.wait()
    i0 = lax.broadcasted_iota(jnp.int32, (2 * LANES, LANES), 0)
    i1 = lax.broadcasted_iota(jnp.int32, (2 * LANES, LANES), 1)
    shift = jnp.where(i0 == i1 + LANES - lag, 1.0, 0.0).astype(jnp.bfloat16)
    tiles = days // LANES
    for j in range(tiles):
        p = (j + tiles - 1) % tiles
        two = jnp.concatenate(
            [rain_v[:, p * LANES:(p + 1) * LANES], rain_v[:, j * LANES:(j + 1) * LANES]], axis=1
        )
        rain_all[z + 1, :, j * LANES:(j + 1) * LANES] = jnp.dot(
            two, shift, preferred_element_type=jnp.float32
        ).astype(jnp.bfloat16)

    def strip_of(chunk, q):
        return rain_all.at[chunk + 1, q * strip:(q + 1) * strip, :]

    edges = [
        rcopy(
            rain_all.at[ZS, q * strip:(q + 1) * strip, 0:LANES],
            rain_all.at[0, q * strip:(q + 1) * strip, 0:LANES],
            se.at[q], re.at[q], far,
        )
        for q in range(4)
    ]

    @pl.when(yh == 0)
    def _():
        rain_all[0, :, 0:LANES] = jnp.zeros((rows, LANES), jnp.bfloat16)

    def pass_edge(chunk, q):
        pl.when((chunk == ZS - 1) & (yh == 0))(edges[q].start)

    def ring_copy(way, q, s):
        chunk = zo_(1 - s) if way == 0 else zo_(s - 1)
        at = strip_of(chunk, q)
        return rcopy(at, at, sr.at[way, q, s - 1], rr.at[way, q, s - 1], ahead if way == 0 else behind)

    def reach(way, q):
        return 4 if (q + way) % 2 == 0 else 3

    def ring_start(q):
        pass_edge(z, q)
        for way in (0, 1):
            send(ring_copy(way, q, 1))

    def ring_arrive(way, q, s):
        chunk = zo_(-s) if way == 0 else zo_(s)
        at = strip_of(chunk, q)
        rcopy(at, at, sr.at[way, q, s - 1], rr.at[way, q, s - 1], behind).wait_recv()
        if s < reach(way, q):
            send(ring_copy(way, q, s + 1))
        pass_edge(chunk, q)

    for q in WAVES[0]:
        ring_start(q)

    for k in ORDER:
        d = lax.rem(x - swap_pair(k) + XS, XS)
        src = stage.at[d]
        rcopy(src, src, s1.at[0], r1.at[d], right).wait_recv()
        dst = cell(z, yl, x)
        remote = rcopy(src, dst, s2.at[k], r2.at[k], swap_dev(k))
        if k == 0:
            send(remote, crossed)
            pl.when(jnp.logical_not(crossed))(pltpu.make_async_copy(src, dst, r2.at[0]).start)
        else:
            send(remote)

    def home(k):
        return 2 * lax.rem(zp - k + 4, 4) + c

    first = yl == other

    def to_sibling(at, j, o):
        send(rcopy(at, at, sc.at[j, o], rc.at[j, o], sibling))

    def along_x(at, j, when=None):
        send(rcopy(at, at, sx.at[0, j], rx.at[0, j], right), when)
        send(rcopy(at, at, sx.at[1, j], rx.at[1, j], left), when)

    def half_of(j):
        return other if j < 4 else yh

    def arrive_own(i):
        k = ORDER[i]
        at = cell(home(k), yl, x)
        rcopy(at, at, s2.at[k], r2.at[k], right).wait_recv()
        send(rcopy(at, at, s3.at[k], r3.at[k], near))
        along_x(at, i, first)
        to_sibling(at, jnp.where(first, i, i + 4), 0)

    def arrive_near(i):
        k = ORDER[i]
        at = cell(home(k), 1 - yl, x)
        rcopy(at, at, s3.at[k], r3.at[k], near).wait_recv()
        j = jnp.where(first, i + 4, i)
        along_x(at, j)
        to_sibling(at, j, 0)

    def late_own(i):
        along_x(cell(home(ORDER[i]), yl, x), i + 4, jnp.logical_not(first))

    def arrive_x(j, o):
        at = cell(home(ORDER[j % 4]), half_of(j), xo({1: 3, 2: 1, 3: 2}[o]))
        rcopy(at, at, sx.at[o - 1, j], rx.at[o - 1, j], right).wait_recv()
        if o == 1 and j % 2 == 0:
            send(rcopy(at, at, sx.at[2, j], rx.at[2, j], right))
        if o == 2 and j % 2 == 1:
            send(rcopy(at, at, sx.at[2, j], rx.at[2, j], left))
        to_sibling(at, j, o)

    def flow_ready(h):
        for j in range(4 * h, 4 * h + 4):
            zd = 2 * lax.rem(zp - ORDER[j % 4] + 4, 4) + (1 - c)
            for o in range(4):
                at = cell(zd, half_of(j), xo((0, 3, 1, 2)[o]))
                rcopy(at, at, sc.at[j, o], rc.at[j, o], sibling).wait_recv()

    lane = lax.broadcasted_iota(jnp.int32, (strip, LANES), 1)

    def folded(v):
        return sum(v[:, t * LANES:(t + 1) * LANES] for t in range(tiles))

    def multiply(q, h):
        at = slice(q * strip, (q + 1) * strip)
        half = other if h == 0 else yh
        acc[h, at, :] = jnp.zeros((strip, rows), jnp.float32)

        def step(zd, carry):
            before = rain_all[zd, at, 0:LANES].astype(jnp.float32)
            here = rain_all[zd + 1, at, 0:LANES].astype(jnp.float32)
            head = jnp.where(lane < lag, before, here).astype(jnp.bfloat16)
            used = jnp.concatenate([head, rain_all[zd + 1, at, LANES:]], axis=1)
            acc[h, at, :] += lax.dot_general(
                used, flow_all[zd, half], (((1,), (1,)), ((), ())), preferred_element_type=jnp.float32
            )
            if h == 0:
                wide = used.astype(jnp.float32)
                rain_part[0, at, :] += folded(wide)
                rain_part[1, at, :] += folded(wide * wide)
            return carry

        lax.fori_loop(0, ZS, step, 0)

    def flow_stats(h):
        half = other if h == 0 else yh
        blocks = rows // LANES
        flow_part[h] = jnp.zeros((2, rows, LANES), jnp.float32)
        lanes = lax.broadcasted_iota(jnp.int32, (LANES, LANES), 1)

        def step(i, carry):
            zd = 2 * lax.div(i, blocks) + c
            at = pl.ds(pl.multiple_of(lax.rem(i, blocks) * LANES, LANES), LANES)
            wide = flow_all[zd, half, at, :].astype(jnp.float32)
            skip = jnp.where((yh == 0) & (zd == 0), lag, 0)
            head = jnp.where(lanes < skip, 0.0, wide[:, 0:LANES])
            wide = jnp.concatenate([head, wide[:, LANES:]], axis=1)
            flow_part[h, 0, at, :] += folded(wide)
            flow_part[h, 1, at, :] += folded(wide * wide)
            return carry

        lax.fori_loop(0, 4 * blocks, step, 0)

    def rows_of(ref, b):
        return jnp.sum(ref[b * LANES:(b + 1) * LANES, :].T, axis=0, keepdims=True)

    def share_stats():
        for b in range(rows // LANES):
            rs, rq = rows_of(rain_part.at[0], b), rows_of(rain_part.at[1], b)
            zero = jnp.zeros((4, LANES), jnp.float32)
            for i, h in ((0, 1), (1, 0)):
                fs, fq = rows_of(flow_part.at[h, 0], b), rows_of(flow_part.at[h, 1], b)
                stat_send[i, :, b * LANES:(b + 1) * LANES] = jnp.concatenate([fs, fq, rs, rq, zero], axis=0)
        for i, (src, to) in enumerate(((0, sibling), (1, far), (1, far_sibling))):
            send(rcopy(stat_send.at[src], stat_recv.at[i], st.at[i], rt.at[i], to))

    def take_stats():
        for i in range(3):
            at = stat_recv.at[i]
            rcopy(at, at, st.at[i], rt.at[i], sibling).wait_recv()
        is_flow = lax.broadcasted_iota(jnp.int32, (8, rows), 0) < 2
        halves = stat_recv[0] + stat_recv[2]
        stat_ref[...] = stat_send[0] + stat_recv[1] + jnp.where(is_flow, halves, 0.0)

    def strip_at(ref, q):
        return ref.at[q * strip:(q + 1) * strip, :]

    def give(q):
        send(rcopy(strip_at(acc.at[0], q), strip_at(relay, q), sg.at[q], rg.at[q], up if q % 2 == 0 else down))

    def hand_on(q):
        at = strip_at(relay, q)
        rcopy(at, at, sg.at[q], rg.at[q], up).wait_recv()
        send(rcopy(at, strip_at(final, q), sf.at[q], rf.at[q], up if q % 2 == 0 else down))

    def finish(q):
        at = slice(q * strip, (q + 1) * strip)
        ref = strip_at(final, q)
        rcopy(ref, ref, sf.at[q], rf.at[q], up).wait_recv()
        cross_ref[at, :] = acc[1, at, :] + final[at, :]

    def edge_ready(q):
        pl.when(yh == 1)(edges[q].wait_recv)

    events = []

    def at_time(t, *calls):
        events.append((t, len(events), calls))

    for i in range(4):
        at_time(9 + 3.3 * i, lambda i=i: arrive_own(i))
        at_time(13 + 3.3 * i, lambda i=i: arrive_near(i))
        at_time(26.5 + 0.1 * i, lambda i=i: late_own(i))
    for j in range(8):
        at_time(16.5 + 4.9 * j, lambda j=j: arrive_x(j, 1), lambda j=j: arrive_x(j, 2))
        at_time(23.5 + 4.9 * j, lambda j=j: arrive_x(j, 3))
    for w, wave in enumerate(WAVES):
        n = 0
        for s in (1, 2, 3, 4):
            for q in wave:
                for way in (0, 1):
                    if s <= reach(way, q):
                        at_time(8 + 3.8 * (7 * w + n), lambda way=way, q=q, s=s: ring_arrive(way, q, s))
                n += 1 if s < 4 else 0.5
                if w + 1 < len(WAVES) and s == 3:
                    at_time(8 + 3.8 * (7 * w + n) - 3, lambda q=WAVES[w + 1][wave.index(q)]: ring_start(q))

    def send_half(wave):
        for q in wave:
            edge_ready(q)
            multiply(q, 0)
            give(q)

    rain_part[...] = jnp.zeros(rain_part.shape, jnp.float32)
    at_time(44, lambda: flow_ready(0), lambda: send_half(WAVES[0]))
    at_time(46, lambda: flow_stats(0))
    at_time(54, *[lambda q=q: hand_on(q) for q in WAVES[0]])
    at_time(100, lambda: send_half(WAVES[1]))
    at_time(101, lambda: flow_ready(1), lambda: flow_stats(1), share_stats)
    at_time(102, *[lambda q=q: multiply(q, 1) for q in WAVES[0]])
    at_time(103, *[lambda q=q: hand_on(q) for q in WAVES[1]])
    at_time(104, *[lambda q=q: multiply(q, 1) for q in WAVES[1]])
    at_time(105, take_stats)
    at_time(106, *[lambda q=q: finish(q) for q in range(4)])

    for _, _, calls in sorted(events, key=lambda e: e[:2]):
        for call in calls:
            call()

    for copy, when in pending:
        if when is None:
            copy.wait_send()
        else:
            pl.when(when)(copy.wait_send)
    for q in range(4):
        pl.when(yh == 0)(edges[q].wait_send)


def local(rainfall, runoff, lag_days):
    rows, days = rainfall.shape
    dma = pltpu.SemaphoreType.DMA
    bf16, f32 = jnp.bfloat16, jnp.float32
    cross, stats = pl.pallas_call(
        kernel,
        out_shape=(jax.ShapeDtypeStruct((rows, rows), f32), jax.ShapeDtypeStruct((8, rows), f32)),
        in_specs=[
            pl.BlockSpec(memory_space=pltpu.SMEM),
            pl.BlockSpec(memory_space=pl.ANY),
            pl.BlockSpec(memory_space=pl.ANY),
        ],
        out_specs=[pl.BlockSpec(memory_space=pltpu.VMEM)] * 2,
        scratch_shapes=[
            pltpu.VMEM((rows, days), bf16),
            pltpu.VMEM((rows, days), bf16),
            pltpu.VMEM((XS, rows // XS, days), bf16),
            pltpu.VMEM((ZS + 1, rows, days), bf16),
            pltpu.VMEM((ZS, 2, rows, days), bf16),
            pltpu.VMEM((2, rows, rows), f32),
            pltpu.VMEM((rows, rows), f32),
            pltpu.VMEM((rows, rows), f32),
            pltpu.VMEM((2, rows, LANES), f32),
            pltpu.VMEM((2, 2, rows, LANES), f32),
            pltpu.VMEM((2, 8, rows), f32),
            pltpu.VMEM((3, 8, rows), f32),
            dma((2,)),
            dma((4,)), dma((4,)),
            dma((4,)), dma((4,)),
            dma((4,)), dma((4,)),
            dma((3, 8)), dma((3, 8)),
            dma((8, 4)), dma((8, 4)),
            dma((2, 4, 4)), dma((2, 4, 4)),
            dma((4,)), dma((4,)),
            dma((4,)), dma((4,)),
            dma((4,)), dma((4,)),
            dma((3,)), dma((3,)),
        ],
        compiler_params=pltpu.CompilerParams(
            collective_id=0, has_side_effects=True, vmem_limit_bytes=48 * 2**20
        ),
        cost_estimate=pl.CostEstimate(
            flops=2 * rows * 2 * rows * ZS * days, bytes_accessed=4 * rows * rows, transcendentals=0
        ),
    )(lag_days, rainfall, runoff)
    total = days * lax.axis_size("tm")
    samples = (total - lag_days[0]).astype(f32)
    flow_sum, flow_square, rain_sum, rain_square = stats[0], stats[1], stats[2], stats[3]
    covar = cross - rain_sum[:, None] * flow_sum[None, :] / samples
    rain_var = rain_square - rain_sum * rain_sum / samples
    flow_var = flow_square - flow_sum * flow_sum / samples
    return covar / jnp.sqrt(rain_var[:, None] * flow_var[None, :])


def solution(mesh):
    placed = (P("blk", "tm"), P("blk", "tm"), P())
    return jax.shard_map(
        local, mesh=mesh, in_specs=placed, out_specs=P("blk", "tm"), check_vma=False
    )
```

```python
import jax
import jax.numpy as jnp
from jax import lax
from jax.experimental import pallas as pl
from jax.experimental.pallas import tpu as pltpu
from jax.sharding import PartitionSpec as P

XS, ZS, LANES = 4, 8, 128
ORDER = (0, 1, 3, 2)
WAVES = ((0, 1), (2, 3), (4, 5))
BOUNDS = (0, 160, 320, 416, 512, 576, 640)
STRIPS = len(BOUNDS) - 1


def kernel(
    lag_ref, rain_ref, flow_ref, cross_ref, stat_ref,
    flow_v, rain_v, stage, rain_all, flow_all, acc, relay, final,
    rain_part, flow_part, stat_send, stat_recv,
    load_sem, s1, r1, s2, r2, s3, r3, sx, rx, sc, rc, sr, rr, se, re, sg, rg, sf, rf, st, rt,
):
    rows, days = rain_v.shape
    piece = rows // XS
    assert rows == BOUNDS[-1]
    lag = lag_ref[0]
    blk, tm = lax.axis_index("blk"), lax.axis_index("tm")
    yl, x, c = lax.div(blk, 8), lax.rem(lax.div(blk, 2), 4), lax.rem(blk, 2)
    yh, z = lax.div(tm, 8), lax.rem(tm, 8)
    zp, zo = lax.div(z, 2), lax.rem(z, 2)
    other = 1 - yh

    def dev(yl_=None, x_=None, c_=None, yh_=None, z_=None):
        b = (yl if yl_ is None else yl_) * 8 + (x if x_ is None else x_) * 2 + (c if c_ is None else c_)
        t = (yh if yh_ is None else yh_) * 8 + (z if z_ is None else z_)
        return (b, t)

    def xo(d):
        return lax.rem(x + d, XS)

    def zo_(d):
        return lax.rem(z + d + ZS, ZS)

    y = 2 * yh + yl
    yu, yd = lax.rem(y + 1, 4), lax.rem(y + 3, 4)
    up = dev(yl_=lax.rem(yu, 2), yh_=lax.div(yu, 2))
    down = dev(yl_=lax.rem(yd, 2), yh_=lax.div(yd, 2))
    near = dev(yl_=1 - yl)
    sibling = dev(c_=1 - c)
    far = dev(yh_=other)
    far_sibling = dev(yh_=other, c_=1 - c)
    right, left = dev(x_=xo(1)), dev(x_=xo(3))
    ahead, behind = dev(z_=zo_(1)), dev(z_=zo_(-1))

    def swap_pair(k):
        return lax.rem(zp + k, 4)

    def swap_dev(k):
        return dev(z_=2 * swap_pair(k) + c, c_=zo)

    def rcopy(src, dst, send, recv, to):
        return pltpu.make_async_remote_copy(
            src_ref=src, dst_ref=dst, send_sem=send, recv_sem=recv,
            device_id=to, device_id_type=pl.DeviceIdType.MESH,
        )

    pending = []

    def send(copy, when=None):
        if when is None:
            copy.start()
        else:
            pl.when(when)(copy.start)
        pending.append((copy, when))

    load_flow = pltpu.make_async_copy(flow_ref, flow_v, load_sem.at[0])
    load_rain = pltpu.make_async_copy(rain_ref, rain_v, load_sem.at[1])
    load_flow.start()
    load_rain.start()

    crossed = c != zo
    barrier = pltpu.get_barrier_semaphore()
    partners = [dev(x_=xo(d)) for d in (1, 2, 3)]
    partners += [ahead, behind, up, down, far, far_sibling, sibling]
    partners += [swap_dev(k) for k in (1, 2, 3)]

    def greet(to):
        pl.semaphore_signal(barrier, inc=1, device_id=to, device_id_type=pl.DeviceIdType.MESH)

    for to in partners:
        greet(to)

    @pl.when(crossed)
    def _():
        greet(swap_dev(0))

    pl.semaphore_wait(barrier, len(partners) + jnp.where(crossed, 1, 0))

    def part(ref, i):
        return ref.at[pl.ds(pl.multiple_of(i * piece, piece), piece), :]

    def cell(zd, half, col):
        return flow_all.at[zd, half, pl.ds(pl.multiple_of(col * piece, piece), piece), :]

    load_flow.wait()
    own = pltpu.make_async_copy(part(flow_v, x), stage.at[0], r1.at[0])
    own.start()
    for d in (1, 3, 2):
        send(rcopy(part(flow_v, xo(d)), stage.at[d], s1.at[d], r1.at[d], dev(x_=xo(d))))

    load_rain.wait()
    i0 = lax.broadcasted_iota(jnp.int32, (2 * LANES, LANES), 0)
    i1 = lax.broadcasted_iota(jnp.int32, (2 * LANES, LANES), 1)
    shift = jnp.where(i0 == i1 + LANES - lag, 1.0, 0.0).astype(jnp.bfloat16)
    tiles = days // LANES
    for j in range(tiles):
        p = (j + tiles - 1) % tiles
        two = jnp.concatenate(
            [rain_v[:, p * LANES:(p + 1) * LANES], rain_v[:, j * LANES:(j + 1) * LANES]], axis=1
        )
        rain_all[z + 1, :, j * LANES:(j + 1) * LANES] = jnp.dot(
            two, shift, preferred_element_type=jnp.float32
        ).astype(jnp.bfloat16)

    def strip_of(chunk, q):
        return rain_all.at[chunk + 1, BOUNDS[q]:BOUNDS[q + 1], :]

    edges = [
        rcopy(
            rain_all.at[ZS, BOUNDS[q]:BOUNDS[q + 1], 0:LANES],
            rain_all.at[0, BOUNDS[q]:BOUNDS[q + 1], 0:LANES],
            se.at[q], re.at[q], far,
        )
        for q in range(STRIPS)
    ]

    @pl.when(yh == 0)
    def _():
        rain_all[0, :, 0:LANES] = jnp.zeros((rows, LANES), jnp.bfloat16)

    def pass_edge(chunk, q):
        pl.when((chunk == ZS - 1) & (yh == 0))(edges[q].start)

    def ring_copy(way, q, s):
        chunk = zo_(1 - s) if way == 0 else zo_(s - 1)
        at = strip_of(chunk, q)
        return rcopy(at, at, sr.at[way, q, s - 1], rr.at[way, q, s - 1], ahead if way == 0 else behind)

    def reach(way, q):
        return 4 if (q + way) % 2 == 0 else 3

    def ring_start(q):
        pass_edge(z, q)
        for way in (0, 1):
            send(ring_copy(way, q, 1))

    def ring_arrive(way, q, s):
        chunk = zo_(-s) if way == 0 else zo_(s)
        at = strip_of(chunk, q)
        rcopy(at, at, sr.at[way, q, s - 1], rr.at[way, q, s - 1], behind).wait_recv()
        if s < reach(way, q):
            send(ring_copy(way, q, s + 1))
        pass_edge(chunk, q)

    ring_start(WAVES[0][0])

    for k in ORDER:
        d = lax.rem(x - swap_pair(k) + XS, XS)
        src = stage.at[d]
        rcopy(src, src, s1.at[0], r1.at[d], right).wait_recv()
        dst = cell(z, yl, x)
        remote = rcopy(src, dst, s2.at[k], r2.at[k], swap_dev(k))
        if k == 0:
            send(remote, crossed)
            pl.when(jnp.logical_not(crossed))(pltpu.make_async_copy(src, dst, r2.at[0]).start)
        else:
            send(remote)

    ring_start(WAVES[0][1])

    def home(k):
        return 2 * lax.rem(zp - k + 4, 4) + c

    first = yl == other

    def to_sibling(at, j, o):
        send(rcopy(at, at, sc.at[j, o], rc.at[j, o], sibling))

    def along_x(at, j, when=None):
        send(rcopy(at, at, sx.at[0, j], rx.at[0, j], right), when)
        send(rcopy(at, at, sx.at[1, j], rx.at[1, j], left), when)

    def half_of(j):
        return other if j < 4 else yh

    def arrive_own(i):
        k = ORDER[i]
        at = cell(home(k), yl, x)
        rcopy(at, at, s2.at[k], r2.at[k], right).wait_recv()
        send(rcopy(at, at, s3.at[k], r3.at[k], near))
        along_x(at, i, first)
        to_sibling(at, jnp.where(first, i, i + 4), 0)

    def arrive_near(i):
        k = ORDER[i]
        at = cell(home(k), 1 - yl, x)
        rcopy(at, at, s3.at[k], r3.at[k], near).wait_recv()
        j = jnp.where(first, i + 4, i)
        along_x(at, j)
        to_sibling(at, j, 0)

    def late_own(i):
        along_x(cell(home(ORDER[i]), yl, x), i + 4, jnp.logical_not(first))

    def arrive_x(j, o):
        at = cell(home(ORDER[j % 4]), half_of(j), xo({1: 3, 2: 1, 3: 2}[o]))
        rcopy(at, at, sx.at[o - 1, j], rx.at[o - 1, j], right).wait_recv()
        if o == 1 and j % 2 == 0:
            send(rcopy(at, at, sx.at[2, j], rx.at[2, j], right))
        if o == 2 and j % 2 == 1:
            send(rcopy(at, at, sx.at[2, j], rx.at[2, j], left))
        to_sibling(at, j, o)

    def flow_ready(h):
        for j in range(4 * h, 4 * h + 4):
            zd = 2 * lax.rem(zp - ORDER[j % 4] + 4, 4) + (1 - c)
            for o in range(4):
                at = cell(zd, half_of(j), xo((0, 3, 1, 2)[o]))
                rcopy(at, at, sc.at[j, o], rc.at[j, o], sibling).wait_recv()

    def folded(v):
        return sum(v[:, t * LANES:(t + 1) * LANES] for t in range(tiles))

    def multiply(lo, hi, h, s, start):
        at = slice(lo, hi)
        half = other if h == 0 else yh
        lane = lax.broadcasted_iota(jnp.int32, (hi - lo, LANES), 1)
        used = []
        chunks = (zo_(s), zo_(1 - s))
        for zd in chunks:
            before = rain_all[zd, at, 0:LANES].astype(jnp.float32)
            here = rain_all[zd + 1, at, 0:LANES].astype(jnp.float32)
            head = jnp.where(lane < lag, before, here).astype(jnp.bfloat16)
            used.append(jnp.concatenate([head, rain_all[zd + 1, at, LANES:]], axis=1))
        product = lax.dot_general(
            jnp.concatenate(used, axis=1),
            jnp.concatenate([flow_all[zd, half] for zd in chunks], axis=1),
            (((1,), (1,)), ((), ())), preferred_element_type=jnp.float32,
        )
        if start:
            acc[h, at, :] = product
        else:
            acc[h, at, :] += product
        if h == 0:
            wide = [u.astype(jnp.float32) for u in used]
            rain_part[0, at, :] += sum(folded(u) for u in wide)
            rain_part[1, at, :] += sum(folded(u * u) for u in wide)

    def flow_stats(h, m):
        half = other if h == 0 else yh
        blocks = rows // LANES
        lanes = lax.broadcasted_iota(jnp.int32, (LANES, LANES), 1)

        def step(i, carry):
            zd = 2 * m + c
            at = pl.ds(pl.multiple_of(i * LANES, LANES), LANES)
            wide = flow_all[zd, half, at, :].astype(jnp.float32)
            skip = jnp.where((yh == 0) & (zd == 0), lag, 0)
            head = jnp.where(lanes < skip, 0.0, wide[:, 0:LANES])
            wide = jnp.concatenate([head, wide[:, LANES:]], axis=1)
            flow_part[h, 0, at, :] += folded(wide)
            flow_part[h, 1, at, :] += folded(wide * wide)
            return carry

        lax.fori_loop(0, blocks, step, 0)

    def rows_of(ref, b):
        return jnp.sum(ref[b * LANES:(b + 1) * LANES, :].T, axis=0, keepdims=True)

    def share_stats():
        for b in range(rows // LANES):
            rs, rq = rows_of(rain_part.at[0], b), rows_of(rain_part.at[1], b)
            zero = jnp.zeros((4, LANES), jnp.float32)
            for i, h in ((0, 1), (1, 0)):
                fs, fq = rows_of(flow_part.at[h, 0], b), rows_of(flow_part.at[h, 1], b)
                stat_send[i, :, b * LANES:(b + 1) * LANES] = jnp.concatenate([fs, fq, rs, rq, zero], axis=0)
        for i, (src, to) in enumerate(((0, sibling), (1, far), (1, far_sibling))):
            send(rcopy(stat_send.at[src], stat_recv.at[i], st.at[i], rt.at[i], to))

    def take_stats():
        for i in range(3):
            at = stat_recv.at[i]
            rcopy(at, at, st.at[i], rt.at[i], sibling).wait_recv()
        is_flow = lax.broadcasted_iota(jnp.int32, (8, rows), 0) < 2
        halves = stat_recv[0] + stat_recv[2]
        stat_ref[...] = stat_send[0] + stat_recv[1] + jnp.where(is_flow, halves, 0.0)

    def strip_at(ref, q):
        return ref.at[BOUNDS[q]:BOUNDS[q + 1], :]

    def give(q):
        send(rcopy(strip_at(acc.at[0], q), strip_at(relay, q), sg.at[q], rg.at[q], up if q % 2 == 0 else down))

    def hand_on(q):
        at = strip_at(relay, q)
        rcopy(at, at, sg.at[q], rg.at[q], up).wait_recv()
        send(rcopy(at, strip_at(final, q), sf.at[q], rf.at[q], up if q % 2 == 0 else down))

    def finish(q):
        at = slice(BOUNDS[q], BOUNDS[q + 1])
        ref = strip_at(final, q)
        rcopy(ref, ref, sf.at[q], rf.at[q], up).wait_recv()
        cross_ref[at, :] = acc[1, at, :] + final[at, :]

    def edge_ready(wave, s):
        for zd in (zo_(s), zo_(1 - s)):

            @pl.when((zd == 0) & (yh == 1))
            def _():
                for q in wave:
                    edges[q].wait_recv()

    events = []

    def at_time(t, *calls):
        events.append((t, len(events), calls))

    for i in range(4):
        at_time(9 + 3.3 * i, lambda i=i: arrive_own(i))
        at_time(13 + 3.3 * i, lambda i=i: arrive_near(i))
        at_time(26.5 + 0.1 * i, lambda i=i: late_own(i))
    for j in range(8):
        at_time(16.5 + 4.9 * j, lambda j=j: arrive_x(j, 1), lambda j=j: arrive_x(j, 2))
        at_time(22.5 + 4.9 * j, lambda j=j: arrive_x(j, 3))

    def give_half(w, s):
        wave = WAVES[w]
        lo, hi = BOUNDS[wave[0]], BOUNDS[wave[1] + 1]
        edge_ready(wave, s)
        multiply(lo, hi, 0, s, s == 1)
        if s == 4:
            for q in wave:
                give(q)

    ring_from, ring_gap = (10, 43, 57.5), (5, 2.1, 1.4)
    for w, wave in enumerate(WAVES):
        n = 0
        for s in (1, 2, 3, 4):
            for q in wave:
                for way in (0, 1):
                    if s <= reach(way, q):
                        at_time(ring_from[w] + ring_gap[w] * n, lambda way=way, q=q, s=s: ring_arrive(way, q, s))
                n += 1 if s < 4 else 0.5
                if w + 1 < len(WAVES) and s == 3:
                    at_time(
                        ring_from[w] + ring_gap[w] * (n - 0.9), lambda q=WAVES[w + 1][wave.index(q)]: ring_start(q)
                    )
            if w > 0:
                at_time(ring_from[w] + ring_gap[w] * (n - 0.5), lambda w=w, s=s: give_half(w, s))

    rain_part[...] = jnp.zeros(rain_part.shape, jnp.float32)
    flow_part[...] = jnp.zeros(flow_part.shape, jnp.float32)
    at_time(39.5, lambda: flow_ready(0))
    for s in (1, 2, 3, 4):
        at_time(39 + 2 * s, lambda s=s: give_half(0, s))
    for m in range(4):
        at_time(49 + 2 * m, lambda m=m: flow_stats(0, m))
    at_time(57, *[lambda q=q: hand_on(q) for q in WAVES[0]])
    at_time(65.5, *[lambda q=q: hand_on(q) for q in WAVES[1]])
    at_time(101, lambda: flow_ready(1))
    for m in range(4):
        at_time(102, lambda m=m: flow_stats(1, m))
    at_time(103, share_stats)
    cut = BOUNDS[WAVES[1][0]]
    for s in (1, 2, 3, 4):
        at_time(104, lambda s=s: multiply(0, cut, 1, s, s == 1))
    at_time(105, *[lambda q=q: hand_on(q) for q in WAVES[2]])
    at_time(106, *[lambda q=q: finish(q) for q in WAVES[0]])
    for s in (1, 2, 3, 4):
        at_time(107, lambda s=s: multiply(cut, rows, 1, s, s == 1))
    at_time(108, *[lambda q=q: finish(q) for q in WAVES[1] + WAVES[2]])
    at_time(109, take_stats)

    for _, _, calls in sorted(events, key=lambda e: e[:2]):
        for call in calls:
            call()

    for copy, when in pending:
        if when is None:
            copy.wait_send()
        else:
            pl.when(when)(copy.wait_send)
    for q in range(STRIPS):
        pl.when(yh == 0)(edges[q].wait_send)


def local(rainfall, runoff, lag_days):
    rows, days = rainfall.shape
    dma = pltpu.SemaphoreType.DMA
    bf16, f32 = jnp.bfloat16, jnp.float32
    cross, stats = pl.pallas_call(
        kernel,
        out_shape=(jax.ShapeDtypeStruct((rows, rows), f32), jax.ShapeDtypeStruct((8, rows), f32)),
        in_specs=[
            pl.BlockSpec(memory_space=pltpu.SMEM),
            pl.BlockSpec(memory_space=pl.ANY),
            pl.BlockSpec(memory_space=pl.ANY),
        ],
        out_specs=[pl.BlockSpec(memory_space=pltpu.VMEM)] * 2,
        scratch_shapes=[
            pltpu.VMEM((rows, days), bf16),
            pltpu.VMEM((rows, days), bf16),
            pltpu.VMEM((XS, rows // XS, days), bf16),
            pltpu.VMEM((ZS + 1, rows, days), bf16),
            pltpu.VMEM((ZS, 2, rows, days), bf16),
            pltpu.VMEM((2, rows, rows), f32),
            pltpu.VMEM((rows, rows), f32),
            pltpu.VMEM((rows, rows), f32),
            pltpu.VMEM((2, rows, LANES), f32),
            pltpu.VMEM((2, 2, rows, LANES), f32),
            pltpu.VMEM((2, 8, rows), f32),
            pltpu.VMEM((3, 8, rows), f32),
            dma((2,)),
            dma((4,)), dma((4,)),
            dma((4,)), dma((4,)),
            dma((4,)), dma((4,)),
            dma((3, 8)), dma((3, 8)),
            dma((8, 4)), dma((8, 4)),
            dma((2, STRIPS, 4)), dma((2, STRIPS, 4)),
            dma((STRIPS,)), dma((STRIPS,)),
            dma((STRIPS,)), dma((STRIPS,)),
            dma((STRIPS,)), dma((STRIPS,)),
            dma((3,)), dma((3,)),
        ],
        compiler_params=pltpu.CompilerParams(
            collective_id=0, has_side_effects=True, vmem_limit_bytes=60 * 2**20
        ),
        cost_estimate=pl.CostEstimate(
            flops=2 * rows * 2 * rows * ZS * days, bytes_accessed=4 * rows * rows, transcendentals=0
        ),
    )(lag_days, rainfall, runoff)
    total = days * lax.axis_size("tm")
    samples = (total - lag_days[0]).astype(f32)
    flow_sum, flow_square, rain_sum, rain_square = stats[0], stats[1], stats[2], stats[3]
    covar = cross - rain_sum[:, None] * flow_sum[None, :] / samples
    rain_var = rain_square - rain_sum * rain_sum / samples
    flow_var = flow_square - flow_sum * flow_sum / samples
    return covar / jnp.sqrt(rain_var[:, None] * flow_var[None, :])


def solution(mesh):
    placed = (P("blk", "tm"), P("blk", "tm"), P())
    return jax.shard_map(
        local, mesh=mesh, in_specs=placed, out_specs=P("blk", "tm"), check_vma=False
    )
```

```python
import jax
import jax.numpy as jnp
from jax import lax
from jax.experimental import pallas as pl
from jax.experimental.pallas import tpu as pltpu
from jax.sharding import PartitionSpec as P

XS, ZS, LANES = 4, 8, 128
ORDER = (0, 1, 3, 2)
BOUNDS = (0, 192, 384, 512, 640)
STRIPS = len(BOUNDS) - 1
(
    SPREAD, ROLL, RING_START, SWAP, RING, ARRIVE_OWN, ARRIVE_NEAR, ARRIVE_X, LATE, MULTIPLY, GIVE, HAND_ON, FSTAT, SHARE, FINISH, TAKE,
) = range(16)
SCHEDULE = (
    (SPREAD,), (ROLL,), (RING_START, 0), (RING_START, 1), (SWAP, 3), (SWAP, 1), (SWAP, 0), (RING, 0, 0, 1),
    (ARRIVE_OWN, 0), (RING, 1, 0, 1), (ARRIVE_OWN, 1), (RING, 1, 0, 2), (ARRIVE_NEAR, 0), (SWAP, 2), (ARRIVE_OWN, 2),
    (ARRIVE_X, 0, 1), (ARRIVE_NEAR, 2), (RING_START, 2), (ARRIVE_X, 0, 2), (RING, 1, 1, 1), (LATE, 0),
    (RING, 0, 0, 2), (ARRIVE_NEAR, 1), (ARRIVE_X, 2, 1), (ARRIVE_OWN, 3), (ARRIVE_X, 0, 3), (ARRIVE_X, 1, 2),
    (RING, 1, 0, 3), (RING, 1, 1, 2), (RING, 0, 2, 1), (ARRIVE_X, 1, 1), (ARRIVE_X, 2, 2), (RING, 0, 1, 1),
    (RING, 0, 0, 3), (RING, 1, 2, 1), (ARRIVE_X, 2, 3), (RING, 1, 1, 3), (ARRIVE_NEAR, 3), (RING, 1, 2, 2),
    (ARRIVE_X, 3, 2), (ARRIVE_X, 1, 3), (LATE, 2), (ARRIVE_X, 3, 3), (RING, 0, 1, 2), (ARRIVE_X, 3, 1),
    (RING_START, 3), (ARRIVE_X, 4, 2), (RING, 1, 1, 4), (LATE, 1), (ARRIVE_X, 4, 1), (RING, 0, 2, 2), (RING, 1, 3, 1),
    (ARRIVE_X, 6, 2), (LATE, 3), (RING, 1, 2, 3), (RING, 0, 1, 3), (RING, 0, 0, 4), (MULTIPLY, 0, 0, 1, 1),
    (MULTIPLY, 0, 0, 4, 4), (ARRIVE_X, 4, 3), (RING, 0, 3, 1), (MULTIPLY, 0, 0, 2, 3), (GIVE, 0), (GIVE, 1),
    (RING, 1, 3, 2), (ARRIVE_X, 5, 2), (ARRIVE_X, 6, 1), (MULTIPLY, 1, 0, 1, 1), (ARRIVE_X, 7, 2), (ARRIVE_X, 5, 1),
    (RING, 0, 3, 2), (ARRIVE_X, 5, 3), (ARRIVE_X, 6, 3), (ARRIVE_X, 7, 1), (RING, 0, 2, 3), (RING, 1, 3, 3),
    (RING, 0, 2, 4), (RING, 0, 3, 3), (ARRIVE_X, 7, 3), (HAND_ON, 0), (HAND_ON, 1), (MULTIPLY, 1, 0, 3, 3),
    (RING, 1, 3, 4), (MULTIPLY, 1, 0, 2, 2), (MULTIPLY, 1, 0, 4, 4), (GIVE, 2), (GIVE, 3), (FSTAT, 0),
    (MULTIPLY, 0, 1, 1, 4), (HAND_ON, 2), (HAND_ON, 3), (FSTAT, 1), (SHARE,), (MULTIPLY, 1, 1, 1, 4), (FINISH, 0),
    (FINISH, 1), (TAKE,), (FINISH, 2), (FINISH, 3),
)


def kernel(
    lag_ref, rain_v, flow_v, cross_ref, stat_ref,
    stage, rain_all, flow_all, acc, relay, final,
    rain_part, flow_part, stat_send, stat_recv,
    s1, r1, s2, r2, s3, r3, sx, rx, sc, rc, sr, rr, se, re, sg, rg, sf, rf, st, rt,
):
    rows, days = rain_v.shape
    piece = rows // XS
    assert rows == BOUNDS[-1]
    tiles = days // LANES
    lag = lag_ref[0]
    blk, tm = lax.axis_index("blk"), lax.axis_index("tm")
    yl, x, c = lax.div(blk, 8), lax.rem(lax.div(blk, 2), 4), lax.rem(blk, 2)
    yh, z = lax.div(tm, 8), lax.rem(tm, 8)
    zp, zo = lax.div(z, 2), lax.rem(z, 2)
    other = 1 - yh

    def dev(yl_=None, x_=None, c_=None, yh_=None, z_=None):
        b = (yl if yl_ is None else yl_) * 8 + (x if x_ is None else x_) * 2 + (c if c_ is None else c_)
        t = (yh if yh_ is None else yh_) * 8 + (z if z_ is None else z_)
        return (b, t)

    def xo(d):
        return lax.rem(x + d, XS)

    def zo_(d):
        return lax.rem(z + d + ZS, ZS)

    y = 2 * yh + yl
    yu, yd = lax.rem(y + 1, 4), lax.rem(y + 3, 4)
    up = dev(yl_=lax.rem(yu, 2), yh_=lax.div(yu, 2))
    down = dev(yl_=lax.rem(yd, 2), yh_=lax.div(yd, 2))
    near = dev(yl_=1 - yl)
    sibling = dev(c_=1 - c)
    far = dev(yh_=other)
    far_sibling = dev(yh_=other, c_=1 - c)
    right, left = dev(x_=xo(1)), dev(x_=xo(3))
    ahead, behind = dev(z_=zo_(1)), dev(z_=zo_(-1))

    def swap_pair(k):
        return lax.rem(zp + k, 4)

    def swap_dev(k):
        return dev(z_=2 * swap_pair(k) + c, c_=zo)

    def rcopy(src, dst, send, recv, to):
        return pltpu.make_async_remote_copy(
            src_ref=src, dst_ref=dst, send_sem=send, recv_sem=recv,
            device_id=to, device_id_type=pl.DeviceIdType.MESH,
        )

    pending = []

    def send(copy, when=None):
        if when is None:
            copy.start()
        else:
            pl.when(when)(copy.start)
        pending.append((copy, when))

    crossed = c != zo
    barrier = pltpu.get_barrier_semaphore()
    partners = [dev(x_=xo(d)) for d in (1, 2, 3)]
    partners += [ahead, behind, up, down, far, far_sibling, sibling]
    partners += [swap_dev(k) for k in (1, 2, 3)]

    def greet(to):
        pl.semaphore_signal(barrier, inc=1, device_id=to, device_id_type=pl.DeviceIdType.MESH)

    for to in partners:
        greet(to)

    @pl.when(crossed)
    def _():
        greet(swap_dev(0))

    pl.semaphore_wait(barrier, len(partners) + jnp.where(crossed, 1, 0))

    def part(ref, i):
        return ref.at[pl.ds(pl.multiple_of(i * piece, piece), piece), :]

    def cell(zd, half, col):
        return flow_all.at[lax.rem(zd, 2), lax.div(zd, 2), half, pl.ds(pl.multiple_of(col * piece, piece), piece), :]

    def spread():
        pltpu.make_async_copy(part(flow_v, x), stage.at[0], r1.at[0]).start()
        for d in (1, 3, 2):
            send(rcopy(part(flow_v, xo(d)), stage.at[d], s1.at[d], r1.at[d], dev(x_=xo(d))))

    def roll():
        i0 = lax.broadcasted_iota(jnp.int32, (2 * LANES, LANES), 0)
        i1 = lax.broadcasted_iota(jnp.int32, (2 * LANES, LANES), 1)
        shift = jnp.where(i0 == i1 + LANES - lag, 1.0, 0.0).astype(jnp.bfloat16)
        for j in range(tiles):
            p = (j + tiles - 1) % tiles
            two = jnp.concatenate(
                [rain_v[:, p * LANES:(p + 1) * LANES], rain_v[:, j * LANES:(j + 1) * LANES]], axis=1
            )
            rain_all[z + 1, :, j * LANES:(j + 1) * LANES] = jnp.dot(
                two, shift, preferred_element_type=jnp.float32
            ).astype(jnp.bfloat16)

    def strip_of(chunk, q):
        return rain_all.at[chunk + 1, BOUNDS[q]:BOUNDS[q + 1], :]

    edges = [
        rcopy(
            rain_all.at[ZS, BOUNDS[q]:BOUNDS[q + 1], 0:LANES],
            rain_all.at[0, BOUNDS[q]:BOUNDS[q + 1], 0:LANES],
            se.at[q], re.at[q], far,
        )
        for q in range(STRIPS)
    ]

    @pl.when(yh == 0)
    def _():
        rain_all[0, :, 0:LANES] = jnp.zeros((rows, LANES), jnp.bfloat16)

    def pass_edge(chunk, q):
        pl.when((chunk == ZS - 1) & (yh == 0))(edges[q].start)

    def ring_copy(way, q, s):
        chunk = zo_(1 - s) if way == 0 else zo_(s - 1)
        at = strip_of(chunk, q)
        return rcopy(at, at, sr.at[way, q, s - 1], rr.at[way, q, s - 1], ahead if way == 0 else behind)

    def reach(way, q):
        return 4 if (q + way) % 2 == 0 else 3

    def ring_start(q):
        pass_edge(z, q)
        for way in (0, 1):
            send(ring_copy(way, q, 1))

    def ring_arrive(way, q, s):
        chunk = zo_(-s) if way == 0 else zo_(s)
        at = strip_of(chunk, q)
        rcopy(at, at, sr.at[way, q, s - 1], rr.at[way, q, s - 1], behind).wait_recv()
        if s < reach(way, q):
            send(ring_copy(way, q, s + 1))
        pass_edge(chunk, q)

    def swap(k):
        d = lax.rem(x - swap_pair(k) + XS, XS)
        src = stage.at[d]
        rcopy(src, src, s1.at[0], r1.at[d], right).wait_recv()
        dst = cell(z, yl, x)
        remote = rcopy(src, dst, s2.at[k], r2.at[k], swap_dev(k))
        if k == 0:
            send(remote, crossed)
            pl.when(jnp.logical_not(crossed))(pltpu.make_async_copy(src, dst, r2.at[0]).start)
        else:
            send(remote)

    def home(k):
        return 2 * lax.rem(zp - k + 4, 4) + c

    first = yl == other

    got = {}

    def sibling_copy(half, o):
        col = xo((0, 3, 1, 2)[o])
        at = flow_all.at[c, :, half, pl.ds(pl.multiple_of(col * piece, piece), piece), :]
        return rcopy(at, at, sc.at[half, o], rc.at[half, o], sibling)

    def to_sibling(group, half, o):
        got[group, o] = got.get((group, o), 0) + 1
        if got[group, o] == 4:
            send(sibling_copy(half, o))

    def along_x(at, j, when=None):
        send(rcopy(at, at, sx.at[0, j], rx.at[0, j], right), when)
        send(rcopy(at, at, sx.at[1, j], rx.at[1, j], left), when)

    def half_of(j):
        return other if j < 4 else yh

    def arrive_own(i):
        k = ORDER[i]
        at = cell(home(k), yl, x)
        rcopy(at, at, s2.at[k], r2.at[k], right).wait_recv()
        send(rcopy(at, at, s3.at[k], r3.at[k], near))
        along_x(at, i, first)
        to_sibling(ARRIVE_OWN, yl, 0)

    def arrive_near(i):
        k = ORDER[i]
        at = cell(home(k), 1 - yl, x)
        rcopy(at, at, s3.at[k], r3.at[k], near).wait_recv()
        along_x(at, i, jnp.logical_not(first))
        to_sibling(ARRIVE_NEAR, 1 - yl, 0)

    def late(i):
        along_x(cell(home(ORDER[i]), yh, x), i + 4)

    def arrive_x(j, o):
        at = cell(home(ORDER[j % 4]), half_of(j), xo({1: 3, 2: 1, 3: 2}[o]))
        rcopy(at, at, sx.at[o - 1, j], rx.at[o - 1, j], right).wait_recv()
        if o == 1 and j % 2 == 0:
            send(rcopy(at, at, sx.at[2, j], rx.at[2, j], right))
        if o == 2 and j % 2 == 1:
            send(rcopy(at, at, sx.at[2, j], rx.at[2, j], left))
        to_sibling(j // 4, half_of(j), o)

    def flow_ready(h):
        half = other if h == 0 else yh
        for o in range(4):
            sibling_copy(half, o).wait_recv()

    def folded(v):
        return sum(v[:, t * LANES:(t + 1) * LANES] for t in range(tiles))

    def multiply(lo, hi, h, low, high, start):
        at = slice(lo, hi)
        half = other if h == 0 else yh
        lane = lax.broadcasted_iota(jnp.int32, (hi - lo, LANES), 1)
        if start:
            for t in range(lo // LANES, hi // LANES):
                acc[h, t] = jnp.zeros((rows, LANES), jnp.float32)

        def step(s, carry):
            used, cells = [], []
            for zd in (zo_(s), zo_(1 - s)):
                before = rain_all[zd, at, 0:LANES].astype(jnp.float32)
                here = rain_all[zd + 1, at, 0:LANES].astype(jnp.float32)
                head = jnp.where(lane < lag, before, here).astype(jnp.bfloat16)
                used.append(jnp.concatenate([head, rain_all[zd + 1, at, LANES:]], axis=1))
                cells.append(flow_all[lax.rem(zd, 2), lax.div(zd, 2), half])
            product = lax.dot_general(
                jnp.concatenate(cells, axis=1), jnp.concatenate(used, axis=1),
                (((1,), (1,)), ((), ())), preferred_element_type=jnp.float32,
            )
            for t in range(lo // LANES, hi // LANES):
                acc[h, t] += product[:, t * LANES - lo:(t + 1) * LANES - lo]
            if h == 0:
                wide = [u.astype(jnp.float32) for u in used]
                rain_part[0, at, :] += sum(folded(u) for u in wide)
                rain_part[1, at, :] += sum(folded(u * u) for u in wide)
            return carry

        lax.fori_loop(low, high + 1, step, 0)

    def flow_stats(h):
        half = other if h == 0 else yh
        blocks = rows // LANES
        lanes = lax.broadcasted_iota(jnp.int32, (LANES, LANES), 1)

        def step(i, carry):
            m = lax.div(i, blocks)
            zd = 2 * m + c
            at = pl.ds(pl.multiple_of(lax.rem(i, blocks) * LANES, LANES), LANES)
            wide = flow_all[c, m, half, at, :].astype(jnp.float32)
            skip = jnp.where((yh == 0) & (zd == 0), lag, 0)
            head = jnp.where(lanes < skip, 0.0, wide[:, 0:LANES])
            wide = jnp.concatenate([head, wide[:, LANES:]], axis=1)
            flow_part[h, 0, at, :] += folded(wide)
            flow_part[h, 1, at, :] += folded(wide * wide)
            return carry

        lax.fori_loop(0, 4 * blocks, step, 0)

    def rows_of(ref, b):
        return jnp.sum(ref[b * LANES:(b + 1) * LANES, :].T, axis=0, keepdims=True)

    def share_stats():
        for b in range(rows // LANES):
            rs, rq = rows_of(rain_part.at[0], b), rows_of(rain_part.at[1], b)
            zero = jnp.zeros((4, LANES), jnp.float32)
            for i, h in ((0, 1), (1, 0)):
                fs, fq = rows_of(flow_part.at[h, 0], b), rows_of(flow_part.at[h, 1], b)
                stat_send[i, :, b * LANES:(b + 1) * LANES] = jnp.concatenate([fs, fq, rs, rq, zero], axis=0)
        for i, (src, to) in enumerate(((0, sibling), (1, far), (1, far_sibling))):
            send(rcopy(stat_send.at[src], stat_recv.at[i], st.at[i], rt.at[i], to))

    def take_stats():
        for i in range(3):
            at = stat_recv.at[i]
            rcopy(at, at, st.at[i], rt.at[i], sibling).wait_recv()
        is_flow = lax.broadcasted_iota(jnp.int32, (8, rows), 0) < 2
        halves = stat_recv[0] + stat_recv[2]
        stat_ref[...] = stat_send[0] + stat_recv[1] + jnp.where(is_flow, halves, 0.0)

    parcels = (((0, 0, rows), (2, 0, 384)), ((1, 0, rows), (2, 384, rows)), ((3, 0, rows),), ((4, 0, rows),))

    def way_of(q):
        return up if q % 2 == 0 else down

    def give(q):
        for n, (t, lo, hi) in enumerate(parcels[q]):
            src, dst = acc.at[0, t, lo:hi, :], relay.at[t, lo:hi, :]
            send(rcopy(src, dst, sg.at[q, n], rg.at[q, n], way_of(q)))

    def hand_on(q):
        for n, (t, lo, hi) in enumerate(parcels[q]):
            at = relay.at[t, lo:hi, :]
            rcopy(at, at, sg.at[q, n], rg.at[q, n], up).wait_recv()
            send(rcopy(at, final.at[t, lo:hi, :], sf.at[q, n], rf.at[q, n], way_of(q)))

    def finish(q):
        for n, (t, lo, hi) in enumerate(parcels[q]):
            ref = final.at[t, lo:hi, :]
            rcopy(ref, ref, sf.at[q, n], rf.at[q, n], up).wait_recv()
            for i in range(lo, hi, LANES):
                block = acc[1, t, i:i + LANES, :] + final[t, i:i + LANES, :]
                cross_ref[t * LANES:(t + 1) * LANES, i:i + LANES] = block.T

    def edge_ready(wave, s):
        for zd in (zo_(s), zo_(1 - s)):

            @pl.when((zd == 0) & (yh == 1))
            def _():
                for q in wave:
                    edges[q].wait_recv()

    seen = set()

    def once(*key):
        new = key not in seen
        seen.add(key)
        return new

    def step(kind, *at):
        if kind in (MULTIPLY, FSTAT):
            h = at[1] if kind == MULTIPLY else at[0]
            if once(FSTAT, h):
                flow_ready(h)
        if kind == MULTIPLY:
            w, h, low, high = at
            for s in range(low, high + 1):
                if once(RING, w, s):
                    edge_ready((2 * w, 2 * w + 1), s)
            multiply(BOUNDS[2 * w], BOUNDS[2 * w + 2], h, low, high, once(MULTIPLY, w, h))
        else:
            steps[kind](*at)

    steps = {
        SPREAD: spread, ROLL: roll, SWAP: swap, RING_START: ring_start, RING: ring_arrive,
        ARRIVE_OWN: arrive_own, ARRIVE_NEAR: arrive_near, LATE: late, ARRIVE_X: arrive_x, FSTAT: flow_stats,
        GIVE: give, HAND_ON: hand_on, SHARE: share_stats, FINISH: finish, TAKE: take_stats,
    }
    def drain():
        for copy, when in pending:
            if when is None:
                copy.wait_send()
            else:
                pl.when(when)(copy.wait_send)
        pending.clear()

    def drain_edges():
        for q in range(STRIPS):
            pl.when(yh == 0)(edges[q].wait_send)

    rain_part[...] = jnp.zeros(rain_part.shape, jnp.float32)
    flow_part[...] = jnp.zeros(flow_part.shape, jnp.float32)
    for item in SCHEDULE:
        if item[0] in (TAKE, FINISH) and once(FINISH):
            drain_edges()
            drain()
        step(*item)

    drain()


def local(rainfall, runoff, lag_days):
    rows, days = rainfall.shape
    dma = pltpu.SemaphoreType.DMA
    bf16, f32 = jnp.bfloat16, jnp.float32
    cross, stats = pl.pallas_call(
        kernel,
        out_shape=(jax.ShapeDtypeStruct((rows, rows), f32), jax.ShapeDtypeStruct((8, rows), f32)),
        in_specs=[
            pl.BlockSpec(memory_space=pltpu.SMEM),
            pl.BlockSpec(memory_space=pltpu.VMEM),
            pl.BlockSpec(memory_space=pltpu.VMEM),
        ],
        out_specs=[pl.BlockSpec(memory_space=pltpu.VMEM)] * 2,
        scratch_shapes=[
            pltpu.VMEM((XS, rows // XS, days), bf16),
            pltpu.VMEM((ZS + 1, rows, days), bf16),
            pltpu.VMEM((2, ZS // 2, 2, rows, days), bf16),
            pltpu.VMEM((2, rows // LANES, rows, LANES), f32),
            pltpu.VMEM((rows // LANES, rows, LANES), f32),
            pltpu.VMEM((rows // LANES, rows, LANES), f32),
            pltpu.VMEM((2, rows, LANES), f32),
            pltpu.VMEM((2, 2, rows, LANES), f32),
            pltpu.VMEM((2, 8, rows), f32),
            pltpu.VMEM((3, 8, rows), f32),
            dma((4,)), dma((4,)),
            dma((4,)), dma((4,)),
            dma((4,)), dma((4,)),
            dma((3, 8)), dma((3, 8)),
            dma((2, 4)), dma((2, 4)),
            dma((2, STRIPS, 4)), dma((2, STRIPS, 4)),
            dma((STRIPS,)), dma((STRIPS,)),
            dma((4, 2)), dma((4, 2)),
            dma((4, 2)), dma((4, 2)),
            dma((3,)), dma((3,)),
        ],
        compiler_params=pltpu.CompilerParams(
            collective_id=0, has_side_effects=True, vmem_limit_bytes=48 * 2**20
        ),
        cost_estimate=pl.CostEstimate(
            flops=2 * rows * 2 * rows * ZS * days, bytes_accessed=4 * rows * rows, transcendentals=0
        ),
    )(lag_days, rainfall, runoff)
    total = days * lax.axis_size("tm")
    samples = (total - lag_days[0]).astype(f32)
    flow_sum, flow_square, rain_sum, rain_square = stats[0], stats[1], stats[2], stats[3]
    covar = cross - rain_sum[:, None] * flow_sum[None, :] / samples
    rain_var = rain_square - rain_sum * rain_sum / samples
    flow_var = flow_square - flow_sum * flow_sum / samples
    return covar / jnp.sqrt(rain_var[:, None] * flow_var[None, :])


def solution(mesh):
    placed = (P("blk", "tm"), P("blk", "tm"), P())
    return jax.shard_map(
        local, mesh=mesh, in_specs=placed, out_specs=P("blk", "tm"), check_vma=False
    )
```

```python
import jax
import jax.numpy as jnp
from jax import lax
from jax.experimental import pallas as pl
from jax.experimental.pallas import tpu as pltpu
from jax.sharding import PartitionSpec as P

XS, ZS, LANES = 4, 8, 128
ORDER = (0, 1, 3, 2)
BOUNDS = (0, 176, 352, 496, 640)
STRIPS = len(BOUNDS) - 1
CUT = 32
(
    SPREAD, ROLL, RING_START, SWAP, RING, ARRIVE_OWN, ARRIVE_NEAR, ARRIVE_X, LATE, MULTIPLY, GIVE, RSTAT, FSTAT, HAND_ON, SHARE, FINISH, TAKE,
) = range(17)
SCHEDULE = (
    (SPREAD,), (ROLL,), (RING_START, 0), (RING_START, 1), (SWAP, 1), (SWAP, 0), (SWAP, 3), (RING, 1, 0, 1), (SWAP, 2),
    (ARRIVE_OWN, 0), (ARRIVE_OWN, 1), (ARRIVE_OWN, 2), (RING, 1, 0, 2), (ARRIVE_NEAR, 0), (ARRIVE_NEAR, 1),
    (RING_START, 2), (ARRIVE_X, 0, 2), (ARRIVE_NEAR, 2), (ARRIVE_X, 0, 1), (RING, 1, 1, 1), (RING, 0, 0, 1),
    (RING, 0, 0, 2), (LATE, 0), (ARRIVE_X, 2, 1), (RING, 0, 2, 1), (ARRIVE_OWN, 3), (RING, 1, 1, 2), (ARRIVE_X, 1, 2),
    (RING, 1, 0, 3), (ARRIVE_X, 0, 3), (RING, 1, 2, 1), (ARRIVE_X, 2, 2), (RING, 0, 1, 1), (ARRIVE_NEAR, 3),
    (RING, 0, 0, 3), (RING, 1, 2, 2), (RING, 1, 1, 3), (ARRIVE_X, 3, 2), (ARRIVE_X, 3, 1), (ARRIVE_X, 2, 3),
    (ARRIVE_X, 1, 1), (LATE, 1), (RING, 1, 2, 3), (ARRIVE_X, 1, 3), (LATE, 2), (RING, 0, 1, 2), (RING_START, 3),
    (RING, 0, 0, 4), (ARRIVE_X, 3, 3), (ARRIVE_X, 4, 1), (RING, 0, 1, 3), (RING, 0, 2, 2), (RING, 1, 1, 4),
    (RING, 1, 3, 1), (ARRIVE_X, 4, 2), (LATE, 3), (MULTIPLY, 0, 0, 4, 4), (MULTIPLY, 0, 0, 1, 1), (RING, 0, 3, 1),
    (MULTIPLY, 0, 0, 2, 3), (RING, 1, 3, 2), (ARRIVE_X, 6, 2), (GIVE, 1), (GIVE, 0), (MULTIPLY, 1, 0, 1, 1),
    (RSTAT, 0), (ARRIVE_X, 4, 3), (ARRIVE_X, 5, 2), (ARRIVE_X, 6, 1), (RING, 0, 3, 2), (ARRIVE_X, 7, 2), (FSTAT, 0),
    (RING, 0, 2, 3), (RING, 1, 3, 3), (HAND_ON, 0), (ARRIVE_X, 6, 3), (HAND_ON, 1), (ARRIVE_X, 5, 1), (RING, 0, 3, 3),
    (ARRIVE_X, 7, 1), (RING, 1, 3, 4), (MULTIPLY, 1, 0, 3, 3), (ARRIVE_X, 7, 3), (ARRIVE_X, 5, 3), (RING, 0, 2, 4),
    (MULTIPLY, 1, 0, 2, 2), (MULTIPLY, 1, 0, 4, 4), (GIVE, 2), (GIVE, 3), (RSTAT, 1), (FSTAT, 1),
    (MULTIPLY, 0, 1, 1, 4), (SHARE,), (HAND_ON, 3), (HAND_ON, 2), (MULTIPLY, 1, 1, 1, 4), (FINISH, 0), (FINISH, 1),
    (FINISH, 3), (TAKE,), (FINISH, 2),
)


def kernel(
    lag_ref, rain_v, flow_v, cross_ref, stat_ref,
    stage, rain_all, flow_all, acc, relay, final,
    rain_part, flow_part, stat_send, stat_recv,
    s1, r1, s2, r2, s3, r3, sx, rx, sc, rc, sr, rr, se, re, sg, rg, sf, rf, st, rt,
):
    rows, days = rain_v.shape
    piece = rows // XS
    assert rows == BOUNDS[-1]
    tiles = days // LANES
    lag = lag_ref[0]
    blk, tm = lax.axis_index("blk"), lax.axis_index("tm")
    yl, x, c = lax.div(blk, 8), lax.rem(lax.div(blk, 2), 4), lax.rem(blk, 2)
    yh, z = lax.div(tm, 8), lax.rem(tm, 8)
    zp, zo = lax.div(z, 2), lax.rem(z, 2)
    other = 1 - yh

    def dev(yl_=None, x_=None, c_=None, yh_=None, z_=None):
        b = (yl if yl_ is None else yl_) * 8 + (x if x_ is None else x_) * 2 + (c if c_ is None else c_)
        t = (yh if yh_ is None else yh_) * 8 + (z if z_ is None else z_)
        return (b, t)

    def xo(d):
        return lax.rem(x + d, XS)

    def zo_(d):
        return lax.rem(z + d + ZS, ZS)

    y = 2 * yh + yl
    yu, yd = lax.rem(y + 1, 4), lax.rem(y + 3, 4)
    up = dev(yl_=lax.rem(yu, 2), yh_=lax.div(yu, 2))
    down = dev(yl_=lax.rem(yd, 2), yh_=lax.div(yd, 2))
    near = dev(yl_=1 - yl)
    sibling = dev(c_=1 - c)
    far = dev(yh_=other)
    far_sibling = dev(yh_=other, c_=1 - c)
    right, left = dev(x_=xo(1)), dev(x_=xo(3))
    ahead, behind = dev(z_=zo_(1)), dev(z_=zo_(-1))

    def swap_pair(k):
        return lax.rem(zp + k, 4)

    def swap_dev(k):
        return dev(z_=2 * swap_pair(k) + c, c_=zo)

    def rcopy(src, dst, send, recv, to):
        return pltpu.make_async_remote_copy(
            src_ref=src, dst_ref=dst, send_sem=send, recv_sem=recv,
            device_id=to, device_id_type=pl.DeviceIdType.MESH,
        )

    pending = []

    def send(copy, when=None):
        if when is None:
            copy.start()
        else:
            pl.when(when)(copy.start)
        pending.append((copy, when))

    crossed = c != zo
    barrier = pltpu.get_barrier_semaphore()
    partners = [dev(x_=xo(d)) for d in (1, 2, 3)]
    partners += [ahead, behind, up, down, far, far_sibling, sibling]
    partners += [swap_dev(k) for k in (1, 2, 3)]

    def greet(to):
        pl.semaphore_signal(barrier, inc=1, device_id=to, device_id_type=pl.DeviceIdType.MESH)

    for to in partners:
        greet(to)

    @pl.when(crossed)
    def _():
        greet(swap_dev(0))

    pl.semaphore_wait(barrier, len(partners) + jnp.where(crossed, 1, 0))

    def part(ref, i):
        return ref.at[pl.ds(pl.multiple_of(i * piece, piece), piece), :]

    def cell(zd, half, col):
        return flow_all.at[lax.rem(zd, 2), lax.div(zd, 2), half, pl.ds(pl.multiple_of(col * piece, piece), piece), :]

    def spread():
        pltpu.make_async_copy(part(flow_v, x), stage.at[0], r1.at[0]).start()
        for d in (1, 3, 2):
            send(rcopy(part(flow_v, xo(d)), stage.at[d], s1.at[d], r1.at[d], dev(x_=xo(d))))

    def roll():
        i0 = lax.broadcasted_iota(jnp.int32, (2 * LANES, LANES), 0)
        i1 = lax.broadcasted_iota(jnp.int32, (2 * LANES, LANES), 1)
        shift = jnp.where(i0 == i1 + LANES - lag, 1.0, 0.0).astype(jnp.bfloat16)
        for j in range(tiles):
            p = (j + tiles - 1) % tiles
            two = jnp.concatenate(
                [rain_v[:, p * LANES:(p + 1) * LANES], rain_v[:, j * LANES:(j + 1) * LANES]], axis=1
            )
            rain_all[z + 1, :, j * LANES:(j + 1) * LANES] = jnp.dot(
                two, shift, preferred_element_type=jnp.float32
            ).astype(jnp.bfloat16)

    def strip_of(chunk, q):
        return rain_all.at[chunk + 1, BOUNDS[q]:BOUNDS[q + 1], :]

    edges = [
        rcopy(
            rain_all.at[ZS, BOUNDS[q]:BOUNDS[q + 1], 0:LANES],
            rain_all.at[0, BOUNDS[q]:BOUNDS[q + 1], 0:LANES],
            se.at[q], re.at[q], far,
        )
        for q in range(STRIPS)
    ]

    @pl.when(yh == 0)
    def _():
        rain_all[0, :, 0:LANES] = jnp.zeros((rows, LANES), jnp.bfloat16)

    def pass_edge(chunk, q):
        pl.when((chunk == ZS - 1) & (yh == 0))(edges[q].start)

    def ring_copy(way, q, s):
        chunk = zo_(1 - s) if way == 0 else zo_(s - 1)
        at = strip_of(chunk, q)
        return rcopy(at, at, sr.at[way, q, s - 1], rr.at[way, q, s - 1], ahead if way == 0 else behind)

    def reach(way, q):
        return 4 if (q + way) % 2 == 0 else 3

    def ring_start(q):
        pass_edge(z, q)
        for way in (0, 1):
            send(ring_copy(way, q, 1))

    def ring_arrive(way, q, s):
        chunk = zo_(-s) if way == 0 else zo_(s)
        at = strip_of(chunk, q)
        rcopy(at, at, sr.at[way, q, s - 1], rr.at[way, q, s - 1], behind).wait_recv()
        if s < reach(way, q):
            send(ring_copy(way, q, s + 1))
        pass_edge(chunk, q)

    def swap(k):
        d = lax.rem(x - swap_pair(k) + XS, XS)
        src = stage.at[d]
        rcopy(src, src, s1.at[0], r1.at[d], right).wait_recv()
        dst = cell(z, yl, x)
        remote = rcopy(src, dst, s2.at[k], r2.at[k], swap_dev(k))
        if k == 0:
            send(remote, crossed)
            pl.when(jnp.logical_not(crossed))(pltpu.make_async_copy(src, dst, r2.at[0]).start)
        else:
            send(remote)

    def home(k):
        return 2 * lax.rem(zp - k + 4, 4) + c

    first = yl == other

    got = {}

    def sibling_copy(half, o):
        col = xo((0, 3, 1, 2)[o])
        at = flow_all.at[c, :, half, pl.ds(pl.multiple_of(col * piece, piece), piece), :]
        return rcopy(at, at, sc.at[half, o], rc.at[half, o], sibling)

    def to_sibling(group, half, o):
        got[group, o] = got.get((group, o), 0) + 1
        if got[group, o] == 4:
            send(sibling_copy(half, o))

    def along_x(at, j, when=None):
        send(rcopy(at, at, sx.at[0, j], rx.at[0, j], right), when)
        send(rcopy(at, at, sx.at[1, j], rx.at[1, j], left), when)

    def half_of(j):
        return other if j < 4 else yh

    def arrive_own(i):
        k = ORDER[i]
        at = cell(home(k), yl, x)
        rcopy(at, at, s2.at[k], r2.at[k], right).wait_recv()
        send(rcopy(at, at, s3.at[k], r3.at[k], near))
        along_x(at, i, first)
        to_sibling(ARRIVE_OWN, yl, 0)

    def arrive_near(i):
        k = ORDER[i]
        at = cell(home(k), 1 - yl, x)
        rcopy(at, at, s3.at[k], r3.at[k], near).wait_recv()
        along_x(at, i, jnp.logical_not(first))
        to_sibling(ARRIVE_NEAR, 1 - yl, 0)

    def late(i):
        along_x(cell(home(ORDER[i]), yh, x), i + 4)

    def arrive_x(j, o):
        at = cell(home(ORDER[j % 4]), half_of(j), xo({1: 3, 2: 1, 3: 2}[o]))
        rcopy(at, at, sx.at[o - 1, j], rx.at[o - 1, j], right).wait_recv()
        if o == 1 and j % 2 == 0:
            send(rcopy(at, at, sx.at[2, j], rx.at[2, j], right))
        if o == 2 and j % 2 == 1:
            send(rcopy(at, at, sx.at[2, j], rx.at[2, j], left))
        to_sibling(j // 4, half_of(j), o)

    def flow_ready(h):
        half = other if h == 0 else yh
        for o in range(4):
            sibling_copy(half, o).wait_recv()

    def folded(v):
        return sum(v[:, t * LANES:(t + 1) * LANES] for t in range(tiles))

    def multiply(lo, hi, h, low, high, start):
        at = slice(lo, hi)
        half = other if h == 0 else yh
        lane = lax.broadcasted_iota(jnp.int32, (hi - lo, LANES), 1)
        if start:
            acc[h, at, :] = jnp.zeros((hi - lo, rows), jnp.float32)

        def step(i, carry):
            s = low + lax.div(i, 2)
            zd = zo_(jnp.where(lax.rem(i, 2) == 0, s, 1 - s))
            before = rain_all[zd, at, 0:LANES].astype(jnp.float32)
            here = rain_all[zd + 1, at, 0:LANES].astype(jnp.float32)
            head = jnp.where(lane < lag, before, here).astype(jnp.bfloat16)
            used = jnp.concatenate([head, rain_all[zd + 1, at, LANES:]], axis=1)
            acc[h, at, :] += lax.dot_general(
                used, flow_all[lax.rem(zd, 2), lax.div(zd, 2), half], (((1,), (1,)), ((), ())), preferred_element_type=jnp.float32
            )
            return carry

        lax.fori_loop(0, 2 * (high - low + 1), step, 0)

    def rain_stats(w):
        lo, hi = BOUNDS[2 * w], BOUNDS[2 * w + 2]
        lane = lax.broadcasted_iota(jnp.int32, (CUT, LANES), 1)

        def step(i, carry):
            zd = lax.rem(i, ZS)
            at = pl.ds(pl.multiple_of(lo + lax.div(i, ZS) * CUT, CUT), CUT)
            before = rain_all[zd, at, 0:LANES].astype(jnp.float32)
            wide = rain_all[zd + 1, at, :].astype(jnp.float32)
            head = jnp.where(lane < lag, before, wide[:, 0:LANES])
            wide = jnp.concatenate([head, wide[:, LANES:]], axis=1)
            rain_part[0, at, :] += folded(wide)
            rain_part[1, at, :] += folded(wide * wide)
            return carry

        lax.fori_loop(0, ZS * (hi - lo) // CUT, step, 0)

    def flow_stats(h):
        half = other if h == 0 else yh
        blocks = rows // LANES
        lanes = lax.broadcasted_iota(jnp.int32, (LANES, LANES), 1)

        def step(i, carry):
            m = lax.div(i, blocks)
            zd = 2 * m + c
            at = pl.ds(pl.multiple_of(lax.rem(i, blocks) * LANES, LANES), LANES)
            wide = flow_all[c, m, half, at, :].astype(jnp.float32)
            skip = jnp.where((yh == 0) & (zd == 0), lag, 0)
            head = jnp.where(lanes < skip, 0.0, wide[:, 0:LANES])
            wide = jnp.concatenate([head, wide[:, LANES:]], axis=1)
            flow_part[h, 0, at, :] += folded(wide)
            flow_part[h, 1, at, :] += folded(wide * wide)
            return carry

        lax.fori_loop(0, 4 * blocks, step, 0)

    def rows_of(ref, b):
        return jnp.sum(ref[b * LANES:(b + 1) * LANES, :].T, axis=0, keepdims=True)

    def share_stats():
        for b in range(rows // LANES):
            rs, rq = rows_of(rain_part.at[0], b), rows_of(rain_part.at[1], b)
            zero = jnp.zeros((4, LANES), jnp.float32)
            for i, h in ((0, 1), (1, 0)):
                fs, fq = rows_of(flow_part.at[h, 0], b), rows_of(flow_part.at[h, 1], b)
                stat_send[i, :, b * LANES:(b + 1) * LANES] = jnp.concatenate([fs, fq, rs, rq, zero], axis=0)
        for i, (src, to) in enumerate(((0, sibling), (1, far), (1, far_sibling))):
            send(rcopy(stat_send.at[src], stat_recv.at[i], st.at[i], rt.at[i], to))

    def take_stats():
        for i in range(3):
            at = stat_recv.at[i]
            rcopy(at, at, st.at[i], rt.at[i], sibling).wait_recv()
        is_flow = lax.broadcasted_iota(jnp.int32, (8, rows), 0) < 2
        halves = stat_recv[0] + stat_recv[2]
        stat_ref[...] = stat_send[0] + stat_recv[1] + jnp.where(is_flow, halves, 0.0)

    def strip_at(ref, q):
        return ref.at[BOUNDS[q]:BOUNDS[q + 1], :]

    def give(q):
        send(rcopy(strip_at(acc.at[0], q), strip_at(relay, q), sg.at[q], rg.at[q], up if q % 2 == 0 else down))

    def hand_on(q):
        at = strip_at(relay, q)
        rcopy(at, at, sg.at[q], rg.at[q], up).wait_recv()
        send(rcopy(at, strip_at(final, q), sf.at[q], rf.at[q], up if q % 2 == 0 else down))

    def finish(q):
        at = slice(BOUNDS[q], BOUNDS[q + 1])
        ref = strip_at(final, q)
        rcopy(ref, ref, sf.at[q], rf.at[q], up).wait_recv()
        cross_ref[at, :] = acc[1, at, :] + final[at, :]

    def edge_ready(wave, s):
        for zd in (zo_(s), zo_(1 - s)):

            @pl.when((zd == 0) & (yh == 1))
            def _():
                for q in wave:
                    edges[q].wait_recv()

    seen = set()

    def once(*key):
        new = key not in seen
        seen.add(key)
        return new

    def step(kind, *at):
        if kind in (MULTIPLY, FSTAT):
            h = at[1] if kind == MULTIPLY else at[0]
            if once(FSTAT, h):
                flow_ready(h)
        if kind in (MULTIPLY, RSTAT):
            w, low, high = (at[0], at[2], at[3]) if kind == MULTIPLY else (at[0], 1, 4)
            for s in range(low, high + 1):
                if once(RING, w, s):
                    edge_ready((2 * w, 2 * w + 1), s)
        if kind == MULTIPLY:
            multiply(BOUNDS[2 * w], BOUNDS[2 * w + 2], h, low, high, once(MULTIPLY, w, h))
        else:
            steps[kind](*at)

    steps = {
        SPREAD: spread, ROLL: roll, SWAP: swap, RING_START: ring_start, RING: ring_arrive,
        ARRIVE_OWN: arrive_own, ARRIVE_NEAR: arrive_near, LATE: late, ARRIVE_X: arrive_x, FSTAT: flow_stats, RSTAT: rain_stats,
        GIVE: give, HAND_ON: hand_on, SHARE: share_stats, FINISH: finish, TAKE: take_stats,
    }
    def drain():
        for copy, when in pending:
            if when is None:
                copy.wait_send()
            else:
                pl.when(when)(copy.wait_send)
        pending.clear()

    def drain_edges():
        for q in range(STRIPS):
            pl.when(yh == 0)(edges[q].wait_send)

    rain_part[...] = jnp.zeros(rain_part.shape, jnp.float32)
    flow_part[...] = jnp.zeros(flow_part.shape, jnp.float32)
    for item in SCHEDULE:
        if item[0] in (TAKE, FINISH) and once(FINISH):
            drain_edges()
            drain()
        step(*item)

    drain()


def local(rainfall, runoff, lag_days):
    rows, days = rainfall.shape
    dma = pltpu.SemaphoreType.DMA
    bf16, f32 = jnp.bfloat16, jnp.float32
    cross, stats = pl.pallas_call(
        kernel,
        out_shape=(jax.ShapeDtypeStruct((rows, rows), f32), jax.ShapeDtypeStruct((8, rows), f32)),
        in_specs=[
            pl.BlockSpec(memory_space=pltpu.SMEM),
            pl.BlockSpec(memory_space=pltpu.VMEM),
            pl.BlockSpec(memory_space=pltpu.VMEM),
        ],
        out_specs=[pl.BlockSpec(memory_space=pltpu.VMEM)] * 2,
        scratch_shapes=[
            pltpu.VMEM((XS, rows // XS, days), bf16),
            pltpu.VMEM((ZS + 1, rows, days), bf16),
            pltpu.VMEM((2, ZS // 2, 2, rows, days), bf16),
            pltpu.VMEM((2, rows, rows), f32),
            pltpu.VMEM((rows, rows), f32),
            pltpu.VMEM((rows, rows), f32),
            pltpu.VMEM((2, rows, LANES), f32),
            pltpu.VMEM((2, 2, rows, LANES), f32),
            pltpu.VMEM((2, 8, rows), f32),
            pltpu.VMEM((3, 8, rows), f32),
            dma((4,)), dma((4,)),
            dma((4,)), dma((4,)),
            dma((4,)), dma((4,)),
            dma((3, 8)), dma((3, 8)),
            dma((2, 4)), dma((2, 4)),
            dma((2, STRIPS, 4)), dma((2, STRIPS, 4)),
            dma((STRIPS,)), dma((STRIPS,)),
            dma((STRIPS,)), dma((STRIPS,)),
            dma((STRIPS,)), dma((STRIPS,)),
            dma((3,)), dma((3,)),
        ],
        compiler_params=pltpu.CompilerParams(
            collective_id=0, has_side_effects=True, vmem_limit_bytes=48 * 2**20
        ),
        cost_estimate=pl.CostEstimate(
            flops=2 * rows * 2 * rows * ZS * days, bytes_accessed=4 * rows * rows, transcendentals=0
        ),
    )(lag_days, rainfall, runoff)
    total = days * lax.axis_size("tm")
    samples = (total - lag_days[0]).astype(f32)
    flow_sum, flow_square, rain_sum, rain_square = stats[0], stats[1], stats[2], stats[3]
    covar = cross - rain_sum[:, None] * flow_sum[None, :] / samples
    rain_var = rain_square - rain_sum * rain_sum / samples
    flow_var = flow_square - flow_sum * flow_sum / samples
    return covar / jnp.sqrt(rain_var[:, None] * flow_var[None, :])


def solution(mesh):
    placed = (P("blk", "tm"), P("blk", "tm"), P())
    return jax.shard_map(
        local, mesh=mesh, in_specs=placed, out_specs=P("blk", "tm"), check_vma=False
    )
```

```python
import jax
import jax.numpy as jnp
from jax import lax
from jax.experimental import pallas as pl
from jax.experimental.pallas import tpu as pltpu
from jax.sharding import PartitionSpec as P

XS, ZS, LANES = 4, 8, 128
ORDER = (0, 1, 3, 2)
BOUNDS = (0, 176, 352, 496, 640)
STRIPS = len(BOUNDS) - 1
CUT = 32
(
    SPREAD, RING_START, SWAP, ARRIVE_OWN, RING, ARRIVE_NEAR, ARRIVE_X, LATE, MULTIPLY, GIVE, FSTAT, RSTAT, HAND_ON, SHARE, TAKE, FINISH,
) = range(16)
SCHEDULE = (
    (SPREAD,), (RING_START, 0), (RING_START, 1), (SWAP, 1), (SWAP, 3), (SWAP, 0), (ARRIVE_OWN, 0), (RING, 1, 0, 1),
    (ARRIVE_OWN, 1), (RING, 1, 1, 1), (SWAP, 2), (ARRIVE_OWN, 2), (ARRIVE_NEAR, 0), (ARRIVE_NEAR, 1), (RING_START, 2),
    (RING, 1, 0, 2), (RING, 0, 0, 1), (ARRIVE_NEAR, 2), (ARRIVE_X, 0, 1), (ARRIVE_X, 0, 2), (LATE, 0),
    (RING, 1, 2, 1), (RING, 1, 1, 2), (ARRIVE_X, 2, 1), (RING, 0, 2, 1), (RING, 0, 0, 2), (ARRIVE_OWN, 3),
    (ARRIVE_X, 1, 2), (ARRIVE_X, 2, 2), (ARRIVE_X, 0, 3), (RING, 1, 0, 3), (RING, 0, 1, 1), (ARRIVE_NEAR, 3),
    (RING, 1, 2, 2), (RING, 1, 1, 3), (RING, 0, 0, 3), (ARRIVE_X, 3, 2), (LATE, 2), (ARRIVE_X, 3, 1),
    (ARRIVE_X, 2, 3), (ARRIVE_X, 1, 1), (RING, 1, 2, 3), (ARRIVE_X, 1, 3), (RING, 0, 1, 2), (RING_START, 3),
    (ARRIVE_X, 3, 3), (RING, 0, 2, 2), (RING, 1, 1, 4), (LATE, 1), (RING, 0, 1, 3), (ARRIVE_X, 4, 1), (RING, 1, 3, 1),
    (LATE, 3), (RING, 0, 0, 4), (ARRIVE_X, 4, 2), (MULTIPLY, 0, 0, 4, 4), (MULTIPLY, 0, 0, 1, 1), (RING, 0, 3, 1),
    (MULTIPLY, 0, 0, 2, 3), (RING, 1, 3, 2), (GIVE, 0), (ARRIVE_X, 6, 2), (GIVE, 1), (MULTIPLY, 1, 0, 1, 1),
    (ARRIVE_X, 5, 2), (ARRIVE_X, 6, 1), (RING, 0, 3, 2), (ARRIVE_X, 7, 2), (RING, 0, 2, 3), (ARRIVE_X, 4, 3),
    (RING, 1, 3, 3), (FSTAT, 0), (ARRIVE_X, 6, 3), (RSTAT, 0), (HAND_ON, 0), (ARRIVE_X, 7, 3), (HAND_ON, 1),
    (RING, 0, 3, 3), (ARRIVE_X, 7, 1), (ARRIVE_X, 5, 1), (RING, 1, 3, 4), (ARRIVE_X, 5, 3), (MULTIPLY, 1, 0, 2, 3),
    (RING, 0, 2, 4), (MULTIPLY, 1, 0, 4, 4), (MULTIPLY, 0, 1, 1, 2), (GIVE, 2), (RSTAT, 1), (GIVE, 3), (FSTAT, 1),
    (SHARE,), (MULTIPLY, 0, 1, 3, 4), (HAND_ON, 3), (HAND_ON, 2), (MULTIPLY, 1, 1, 1, 4), (TAKE,), (FINISH, 1),
    (FINISH, 0), (FINISH, 3), (FINISH, 2),
)


def kernel(
    lag_ref, rain_v, flow_v, cross_ref, stat_ref,
    stage, rain_all, flow_all, acc, relay, final,
    rain_part, flow_part, stat_send, stat_recv,
    s1, r1, s2, r2, s3, r3, sx, rx, sc, rc, sr, rr, se, re, sg, rg, sf, rf, st, rt,
):
    rows, days = rain_v.shape
    piece = rows // XS
    assert rows == BOUNDS[-1]
    tiles = days // LANES
    lag = lag_ref[0]
    blk, tm = lax.axis_index("blk"), lax.axis_index("tm")
    yl, x, c = lax.div(blk, 8), lax.rem(lax.div(blk, 2), 4), lax.rem(blk, 2)
    yh, z = lax.div(tm, 8), lax.rem(tm, 8)
    zp, zo = lax.div(z, 2), lax.rem(z, 2)
    other = 1 - yh

    def dev(yl_=None, x_=None, c_=None, yh_=None, z_=None):
        b = (yl if yl_ is None else yl_) * 8 + (x if x_ is None else x_) * 2 + (c if c_ is None else c_)
        t = (yh if yh_ is None else yh_) * 8 + (z if z_ is None else z_)
        return (b, t)

    def xo(d):
        return lax.rem(x + d, XS)

    def zo_(d):
        return lax.rem(z + d + ZS, ZS)

    y = 2 * yh + yl
    yu, yd = lax.rem(y + 1, 4), lax.rem(y + 3, 4)
    up = dev(yl_=lax.rem(yu, 2), yh_=lax.div(yu, 2))
    down = dev(yl_=lax.rem(yd, 2), yh_=lax.div(yd, 2))
    near = dev(yl_=1 - yl)
    sibling = dev(c_=1 - c)
    far = dev(yh_=other)
    far_sibling = dev(yh_=other, c_=1 - c)
    right, left = dev(x_=xo(1)), dev(x_=xo(3))
    ahead, behind = dev(z_=zo_(1)), dev(z_=zo_(-1))

    def swap_pair(k):
        return lax.rem(zp + k, 4)

    def swap_dev(k):
        return dev(z_=2 * swap_pair(k) + c, c_=zo)

    def rcopy(src, dst, send, recv, to):
        return pltpu.make_async_remote_copy(
            src_ref=src, dst_ref=dst, send_sem=send, recv_sem=recv,
            device_id=to, device_id_type=pl.DeviceIdType.MESH,
        )

    pending = []

    def send(copy, when=None):
        if when is None:
            copy.start()
        else:
            pl.when(when)(copy.start)
        pending.append((copy, when))

    crossed = c != zo
    barrier = pltpu.get_barrier_semaphore()
    partners = [dev(x_=xo(d)) for d in (1, 2, 3)]
    partners += [ahead, behind, up, down, far, far_sibling, sibling]
    partners += [swap_dev(k) for k in (1, 2, 3)]

    def greet(to):
        pl.semaphore_signal(barrier, inc=1, device_id=to, device_id_type=pl.DeviceIdType.MESH)

    for to in partners:
        greet(to)

    @pl.when(crossed)
    def _():
        greet(swap_dev(0))

    def part(ref, i):
        return ref.at[pl.ds(pl.multiple_of(i * piece, piece), piece), :]

    def cell(zd, half, col):
        return flow_all.at[lax.rem(zd, 2), lax.div(zd, 2), half, pl.ds(pl.multiple_of(col * piece, piece), piece), :]

    def spread():
        pltpu.make_async_copy(part(flow_v, x), stage.at[0], r1.at[0]).start()
        for d in (1, 3, 2):
            send(rcopy(part(flow_v, xo(d)), stage.at[d], s1.at[d], r1.at[d], dev(x_=xo(d))))

    def roll():
        i0 = lax.broadcasted_iota(jnp.int32, (2 * LANES, LANES), 0)
        i1 = lax.broadcasted_iota(jnp.int32, (2 * LANES, LANES), 1)
        shift = jnp.where(i0 == i1 + LANES - lag, 1.0, 0.0).astype(jnp.bfloat16)
        for j in range(tiles):
            p = (j + tiles - 1) % tiles
            two = jnp.concatenate(
                [rain_v[:, p * LANES:(p + 1) * LANES], rain_v[:, j * LANES:(j + 1) * LANES]], axis=1
            )
            rain_all[z + 1, :, j * LANES:(j + 1) * LANES] = jnp.dot(
                two, shift, preferred_element_type=jnp.float32
            ).astype(jnp.bfloat16)

    def strip_of(chunk, q):
        return rain_all.at[chunk + 1, BOUNDS[q]:BOUNDS[q + 1], :]

    edges = [
        rcopy(
            rain_all.at[ZS, BOUNDS[q]:BOUNDS[q + 1], 0:LANES],
            rain_all.at[0, BOUNDS[q]:BOUNDS[q + 1], 0:LANES],
            se.at[q], re.at[q], far,
        )
        for q in range(STRIPS)
    ]

    @pl.when(yh == 0)
    def _():
        rain_all[0, :, 0:LANES] = jnp.zeros((rows, LANES), jnp.bfloat16)

    def pass_edge(chunk, q):
        pl.when((chunk == ZS - 1) & (yh == 0))(edges[q].start)

    def ring_copy(way, q, s):
        chunk = zo_(1 - s) if way == 0 else zo_(s - 1)
        at = strip_of(chunk, q)
        return rcopy(at, at, sr.at[way, q, s - 1], rr.at[way, q, s - 1], ahead if way == 0 else behind)

    def reach(way, q):
        return 4 if (q + way) % 2 == 0 else 3

    def ring_start(q):
        pass_edge(z, q)
        for way in (0, 1):
            send(ring_copy(way, q, 1))

    def ring_arrive(way, q, s):
        chunk = zo_(-s) if way == 0 else zo_(s)
        at = strip_of(chunk, q)
        rcopy(at, at, sr.at[way, q, s - 1], rr.at[way, q, s - 1], behind).wait_recv()
        if s < reach(way, q):
            send(ring_copy(way, q, s + 1))
        pass_edge(chunk, q)

    def swap(k):
        d = lax.rem(x - swap_pair(k) + XS, XS)
        src = stage.at[d]
        rcopy(src, src, s1.at[0], r1.at[d], right).wait_recv()
        dst = cell(z, yl, x)
        remote = rcopy(src, dst, s2.at[k], r2.at[k], swap_dev(k))
        if k == 0:
            send(remote, crossed)
            pl.when(jnp.logical_not(crossed))(pltpu.make_async_copy(src, dst, r2.at[0]).start)
        else:
            send(remote)

    def home(k):
        return 2 * lax.rem(zp - k + 4, 4) + c

    first = yl == other

    got = {}

    def sibling_copy(half, o):
        col = xo((0, 3, 1, 2)[o])
        at = flow_all.at[c, :, half, pl.ds(pl.multiple_of(col * piece, piece), piece), :]
        return rcopy(at, at, sc.at[half, o], rc.at[half, o], sibling)

    def to_sibling(group, half, o):
        got[group, o] = got.get((group, o), 0) + 1
        if got[group, o] == 4:
            send(sibling_copy(half, o))

    def along_x(at, j, when=None):
        send(rcopy(at, at, sx.at[0, j], rx.at[0, j], right), when)
        send(rcopy(at, at, sx.at[1, j], rx.at[1, j], left), when)

    def half_of(j):
        return other if j < 4 else yh

    def arrive_own(i):
        k = ORDER[i]
        at = cell(home(k), yl, x)
        rcopy(at, at, s2.at[k], r2.at[k], right).wait_recv()
        send(rcopy(at, at, s3.at[k], r3.at[k], near))
        along_x(at, i, first)
        to_sibling(ARRIVE_OWN, yl, 0)

    def arrive_near(i):
        k = ORDER[i]
        at = cell(home(k), 1 - yl, x)
        rcopy(at, at, s3.at[k], r3.at[k], near).wait_recv()
        along_x(at, i, jnp.logical_not(first))
        to_sibling(ARRIVE_NEAR, 1 - yl, 0)

    def late(i):
        along_x(cell(home(ORDER[i]), yh, x), i + 4)

    def arrive_x(j, o):
        at = cell(home(ORDER[j % 4]), half_of(j), xo({1: 3, 2: 1, 3: 2}[o]))
        rcopy(at, at, sx.at[o - 1, j], rx.at[o - 1, j], right).wait_recv()
        if o == 1 and j % 2 == 0:
            send(rcopy(at, at, sx.at[2, j], rx.at[2, j], right))
        if o == 2 and j % 2 == 1:
            send(rcopy(at, at, sx.at[2, j], rx.at[2, j], left))
        to_sibling(j // 4, half_of(j), o)

    def flow_ready(h):
        half = other if h == 0 else yh
        for o in range(4):
            sibling_copy(half, o).wait_recv()

    def folded(v):
        return sum(v[:, t * LANES:(t + 1) * LANES] for t in range(tiles))

    def multiply(lo, hi, h, low, high, start):
        at = slice(lo, hi)
        half = other if h == 0 else yh
        lane = lax.broadcasted_iota(jnp.int32, (hi - lo, LANES), 1)
        if start:
            acc[h, at, :] = jnp.zeros((hi - lo, rows), jnp.float32)

        def step(i, carry):
            s = low + lax.div(i, 2)
            zd = zo_(jnp.where(lax.rem(i, 2) == 0, s, 1 - s))
            before = rain_all[zd, at, 0:LANES].astype(jnp.float32)
            here = rain_all[zd + 1, at, 0:LANES].astype(jnp.float32)
            head = jnp.where(lane < lag, before, here).astype(jnp.bfloat16)
            used = jnp.concatenate([head, rain_all[zd + 1, at, LANES:]], axis=1)
            acc[h, at, :] += lax.dot_general(
                used, flow_all[lax.rem(zd, 2), lax.div(zd, 2), half], (((1,), (1,)), ((), ())), preferred_element_type=jnp.float32
            )
            return carry

        lax.fori_loop(0, 2 * (high - low + 1), step, 0)

    def rain_stats(w):
        lo, hi = BOUNDS[2 * w], BOUNDS[2 * w + 2]
        lane = lax.broadcasted_iota(jnp.int32, (CUT, LANES), 1)

        def step(i, carry):
            zd = lax.rem(i, ZS)
            at = pl.ds(pl.multiple_of(lo + lax.div(i, ZS) * CUT, CUT), CUT)
            before = rain_all[zd, at, 0:LANES].astype(jnp.float32)
            wide = rain_all[zd + 1, at, :].astype(jnp.float32)
            head = jnp.where(lane < lag, before, wide[:, 0:LANES])
            wide = jnp.concatenate([head, wide[:, LANES:]], axis=1)
            rain_part[0, at, :] += folded(wide)
            rain_part[1, at, :] += folded(wide * wide)
            return carry

        lax.fori_loop(0, ZS * (hi - lo) // CUT, step, 0)

    def flow_stats(h):
        half = other if h == 0 else yh
        blocks = rows // LANES
        lanes = lax.broadcasted_iota(jnp.int32, (LANES, LANES), 1)

        def step(i, carry):
            m = lax.div(i, blocks)
            zd = 2 * m + c
            at = pl.ds(pl.multiple_of(lax.rem(i, blocks) * LANES, LANES), LANES)
            wide = flow_all[c, m, half, at, :].astype(jnp.float32)
            skip = jnp.where((yh == 0) & (zd == 0), lag, 0)
            head = jnp.where(lanes < skip, 0.0, wide[:, 0:LANES])
            wide = jnp.concatenate([head, wide[:, LANES:]], axis=1)
            flow_part[h, 0, at, :] += folded(wide)
            flow_part[h, 1, at, :] += folded(wide * wide)
            return carry

        lax.fori_loop(0, 4 * blocks, step, 0)

    def rows_of(ref, b):
        return jnp.sum(ref[b * LANES:(b + 1) * LANES, :].T, axis=0, keepdims=True)

    def share_stats():
        for b in range(rows // LANES):
            rs, rq = rows_of(rain_part.at[0], b), rows_of(rain_part.at[1], b)
            zero = jnp.zeros((4, LANES), jnp.float32)
            for i, h in ((0, 1), (1, 0)):
                fs, fq = rows_of(flow_part.at[h, 0], b), rows_of(flow_part.at[h, 1], b)
                stat_send[i, :, b * LANES:(b + 1) * LANES] = jnp.concatenate([fs, fq, rs, rq, zero], axis=0)
        for i, (src, to) in enumerate(((0, sibling), (1, far), (1, far_sibling))):
            send(rcopy(stat_send.at[src], stat_recv.at[i], st.at[i], rt.at[i], to))

    def take_stats():
        for i in range(3):
            at = stat_recv.at[i]
            rcopy(at, at, st.at[i], rt.at[i], sibling).wait_recv()
        is_flow = lax.broadcasted_iota(jnp.int32, (8, rows), 0) < 2
        halves = stat_recv[0] + stat_recv[2]
        stat_ref[...] = stat_send[0] + stat_recv[1] + jnp.where(is_flow, halves, 0.0)

    def strip_at(ref, q):
        return ref.at[BOUNDS[q]:BOUNDS[q + 1], :]

    def give(q):
        send(rcopy(strip_at(acc.at[0], q), strip_at(relay, q), sg.at[q], rg.at[q], up if q % 2 == 0 else down))

    def hand_on(q):
        at = strip_at(relay, q)
        rcopy(at, at, sg.at[q], rg.at[q], up).wait_recv()
        send(rcopy(at, strip_at(final, q), sf.at[q], rf.at[q], up if q % 2 == 0 else down))

    def finish(q):
        at = slice(BOUNDS[q], BOUNDS[q + 1])
        ref = strip_at(final, q)
        rcopy(ref, ref, sf.at[q], rf.at[q], up).wait_recv()
        cross_ref[at, :] = acc[1, at, :] + final[at, :]

    def edge_ready(wave, s):
        for zd in (zo_(s), zo_(1 - s)):

            @pl.when((zd == 0) & (yh == 1))
            def _():
                for q in wave:
                    edges[q].wait_recv()

    seen = set()

    def once(*key):
        new = key not in seen
        seen.add(key)
        return new

    def step(kind, *at):
        if kind in (MULTIPLY, FSTAT):
            h = at[1] if kind == MULTIPLY else at[0]
            if once(FSTAT, h):
                flow_ready(h)
        if kind in (MULTIPLY, RSTAT):
            w, low, high = (at[0], at[2], at[3]) if kind == MULTIPLY else (at[0], 1, 4)
            for s in range(low, high + 1):
                if once(RING, w, s):
                    edge_ready((2 * w, 2 * w + 1), s)
        if kind == MULTIPLY:
            multiply(BOUNDS[2 * w], BOUNDS[2 * w + 2], h, low, high, once(MULTIPLY, w, h))
        else:
            steps[kind](*at)

    steps = {
        SPREAD: spread, SWAP: swap, RING_START: ring_start, RING: ring_arrive,
        ARRIVE_OWN: arrive_own, ARRIVE_NEAR: arrive_near, LATE: late, ARRIVE_X: arrive_x, FSTAT: flow_stats, RSTAT: rain_stats,
        GIVE: give, HAND_ON: hand_on, SHARE: share_stats, FINISH: finish, TAKE: take_stats,
    }
    def drain():
        for copy, when in pending:
            if when is None:
                copy.wait_send()
            else:
                pl.when(when)(copy.wait_send)
        pending.clear()

    def drain_edges():
        for q in range(STRIPS):
            pl.when(yh == 0)(edges[q].wait_send)

    rain_part[...] = jnp.zeros(rain_part.shape, jnp.float32)
    flow_part[...] = jnp.zeros(flow_part.shape, jnp.float32)
    roll()
    pl.semaphore_wait(barrier, len(partners) + jnp.where(crossed, 1, 0))
    for item in SCHEDULE:
        if item[0] in (TAKE, FINISH) and once(FINISH):
            drain_edges()
            drain()
        step(*item)

    drain()


def local(rainfall, runoff, lag_days):
    rows, days = rainfall.shape
    dma = pltpu.SemaphoreType.DMA
    bf16, f32 = jnp.bfloat16, jnp.float32
    cross, stats = pl.pallas_call(
        kernel,
        out_shape=(jax.ShapeDtypeStruct((rows, rows), f32), jax.ShapeDtypeStruct((8, rows), f32)),
        in_specs=[
            pl.BlockSpec(memory_space=pltpu.SMEM),
            pl.BlockSpec(memory_space=pltpu.VMEM),
            pl.BlockSpec(memory_space=pltpu.VMEM),
        ],
        out_specs=[pl.BlockSpec(memory_space=pltpu.VMEM)] * 2,
        scratch_shapes=[
            pltpu.VMEM((XS, rows // XS, days), bf16),
            pltpu.VMEM((ZS + 1, rows, days), bf16),
            pltpu.VMEM((2, ZS // 2, 2, rows, days), bf16),
            pltpu.VMEM((2, rows, rows), f32),
            pltpu.VMEM((rows, rows), f32),
            pltpu.VMEM((rows, rows), f32),
            pltpu.VMEM((2, rows, LANES), f32),
            pltpu.VMEM((2, 2, rows, LANES), f32),
            pltpu.VMEM((2, 8, rows), f32),
            pltpu.VMEM((3, 8, rows), f32),
            dma((4,)), dma((4,)),
            dma((4,)), dma((4,)),
            dma((4,)), dma((4,)),
            dma((3, 8)), dma((3, 8)),
            dma((2, 4)), dma((2, 4)),
            dma((2, STRIPS, 4)), dma((2, STRIPS, 4)),
            dma((STRIPS,)), dma((STRIPS,)),
            dma((STRIPS,)), dma((STRIPS,)),
            dma((STRIPS,)), dma((STRIPS,)),
            dma((3,)), dma((3,)),
        ],
        compiler_params=pltpu.CompilerParams(
            collective_id=0, has_side_effects=True, vmem_limit_bytes=48 * 2**20
        ),
        cost_estimate=pl.CostEstimate(
            flops=2 * rows * 2 * rows * ZS * days, bytes_accessed=4 * rows * rows, transcendentals=0
        ),
    )(lag_days, rainfall, runoff)
    total = days * lax.axis_size("tm")
    samples = (total - lag_days[0]).astype(f32)
    flow_sum, flow_square, rain_sum, rain_square = stats[0], stats[1], stats[2], stats[3]
    covar = cross - rain_sum[:, None] * flow_sum[None, :] / samples
    rain_var = rain_square - rain_sum * rain_sum / samples
    flow_var = flow_square - flow_sum * flow_sum / samples
    return covar / jnp.sqrt(rain_var[:, None] * flow_var[None, :])


def solution(mesh):
    placed = (P("blk", "tm"), P("blk", "tm"), P())
    return jax.shard_map(
        local, mesh=mesh, in_specs=placed, out_specs=P("blk", "tm"), check_vma=False
    )
```

```python
import jax
import jax.numpy as jnp
from jax import lax
from jax.experimental import pallas as pl
from jax.experimental.pallas import tpu as pltpu
from jax.sharding import PartitionSpec as P

XS, ZS, LANES = 4, 8, 128
ORDER = (0, 1, 3, 2)
BOUNDS = (0, 176, 352, 496, 640)
STRIPS = len(BOUNDS) - 1
CUT = 32
(
    SPREAD, RING_START, SWAP, RING, ARRIVE_OWN, ARRIVE_NEAR, ARRIVE_X, LATE, MULTIPLY, GIVE, FSTAT, RSTAT, HAND_ON, SHARE, FINISH, TAKE,
) = range(16)
SCHEDULE = (
    (SPREAD,), (RING_START, 0), (RING_START, 1), (SWAP, 1), (SWAP, 0), (SWAP, 3), (RING, 1, 0, 1), (SWAP, 2),
    (ARRIVE_OWN, 0), (ARRIVE_OWN, 1), (ARRIVE_OWN, 2), (RING, 1, 0, 2), (RING, 0, 0, 1), (ARRIVE_NEAR, 0),
    (ARRIVE_NEAR, 1), (RING_START, 2), (ARRIVE_X, 0, 2), (ARRIVE_NEAR, 2), (ARRIVE_X, 0, 1), (RING, 1, 1, 1),
    (RING, 0, 0, 2), (LATE, 0), (ARRIVE_X, 2, 1), (RING, 0, 2, 1), (ARRIVE_OWN, 3), (RING, 1, 1, 2), (ARRIVE_X, 1, 2),
    (RING, 1, 0, 3), (RING, 1, 2, 1), (ARRIVE_X, 2, 2), (RING, 0, 1, 1), (ARRIVE_X, 0, 3), (ARRIVE_NEAR, 3),
    (RING, 0, 0, 3), (RING, 1, 2, 2), (RING, 1, 1, 3), (ARRIVE_X, 3, 2), (LATE, 2), (ARRIVE_X, 3, 1),
    (ARRIVE_X, 2, 3), (ARRIVE_X, 1, 1), (RING, 1, 2, 3), (ARRIVE_X, 1, 3), (RING, 0, 1, 2), (RING_START, 3),
    (ARRIVE_X, 3, 3), (RING, 0, 1, 3), (RING, 0, 2, 2), (RING, 1, 1, 4), (LATE, 1), (ARRIVE_X, 4, 1), (RING, 1, 3, 1),
    (ARRIVE_X, 4, 2), (RING, 0, 0, 4), (LATE, 3), (MULTIPLY, 0, 0, 4, 4), (MULTIPLY, 0, 0, 1, 1), (RING, 0, 3, 1),
    (MULTIPLY, 0, 0, 2, 3), (RING, 1, 3, 2), (ARRIVE_X, 6, 2), (GIVE, 1), (GIVE, 0), (MULTIPLY, 1, 0, 1, 1),
    (ARRIVE_X, 5, 2), (ARRIVE_X, 6, 1), (RING, 0, 3, 2), (ARRIVE_X, 7, 2), (RING, 0, 2, 3), (ARRIVE_X, 4, 3),
    (FSTAT, 0), (RING, 1, 3, 3), (ARRIVE_X, 6, 3), (RSTAT, 0), (HAND_ON, 0), (ARRIVE_X, 7, 3), (ARRIVE_X, 5, 3),
    (RING, 0, 3, 3), (HAND_ON, 1), (ARRIVE_X, 7, 1), (ARRIVE_X, 5, 1), (RING, 1, 3, 4), (MULTIPLY, 1, 0, 2, 3),
    (RING, 0, 2, 4), (MULTIPLY, 1, 0, 4, 4), (GIVE, 2), (RSTAT, 1), (GIVE, 3), (FSTAT, 1), (MULTIPLY, 0, 1, 1, 4),
    (SHARE,), (HAND_ON, 3), (HAND_ON, 2), (FINISH, 1), (FINISH, 0), (MULTIPLY, 1, 1, 1, 4), (TAKE,), (FINISH, 2),
    (FINISH, 3),
)


def kernel(
    lag_ref, rain_v, flow_v, cross_ref, stat_ref,
    stage, rain_all, flow_all, acc, relay, final,
    rain_part, flow_part, stat_send, stat_recv,
    s1, r1, s2, r2, s3, r3, sx, rx, sc, rc, sr, rr, se, re, sg, rg, sf, rf, st, rt,
):
    rows, days = rain_v.shape
    piece = rows // XS
    assert rows == BOUNDS[-1]
    tiles = days // LANES
    lag = lag_ref[0]
    blk, tm = lax.axis_index("blk"), lax.axis_index("tm")
    yl, x, c = lax.div(blk, 8), lax.rem(lax.div(blk, 2), 4), lax.rem(blk, 2)
    yh, z = lax.div(tm, 8), lax.rem(tm, 8)
    zp, zo = lax.div(z, 2), lax.rem(z, 2)
    other = 1 - yh

    def dev(yl_=None, x_=None, c_=None, yh_=None, z_=None):
        b = (yl if yl_ is None else yl_) * 8 + (x if x_ is None else x_) * 2 + (c if c_ is None else c_)
        t = (yh if yh_ is None else yh_) * 8 + (z if z_ is None else z_)
        return (b, t)

    def xo(d):
        return lax.rem(x + d, XS)

    def zo_(d):
        return lax.rem(z + d + ZS, ZS)

    y = 2 * yh + yl
    yu, yd = lax.rem(y + 1, 4), lax.rem(y + 3, 4)
    up = dev(yl_=lax.rem(yu, 2), yh_=lax.div(yu, 2))
    down = dev(yl_=lax.rem(yd, 2), yh_=lax.div(yd, 2))
    near = dev(yl_=1 - yl)
    sibling = dev(c_=1 - c)
    far = dev(yh_=other)
    far_sibling = dev(yh_=other, c_=1 - c)
    right, left = dev(x_=xo(1)), dev(x_=xo(3))
    ahead, behind = dev(z_=zo_(1)), dev(z_=zo_(-1))

    def swap_pair(k):
        return lax.rem(zp + k, 4)

    def swap_dev(k):
        return dev(z_=2 * swap_pair(k) + c, c_=zo)

    def rcopy(src, dst, send, recv, to):
        return pltpu.make_async_remote_copy(
            src_ref=src, dst_ref=dst, send_sem=send, recv_sem=recv,
            device_id=to, device_id_type=pl.DeviceIdType.MESH,
        )

    pending = []

    def send(copy, when=None):
        if when is None:
            copy.start()
        else:
            pl.when(when)(copy.start)
        pending.append((copy, when))

    crossed = c != zo
    barrier = pltpu.get_barrier_semaphore()
    partners = [dev(x_=xo(d)) for d in (1, 2, 3)]
    partners += [ahead, behind, up, down, far, far_sibling, sibling]
    partners += [swap_dev(k) for k in (1, 2, 3)]

    def greet(to):
        pl.semaphore_signal(barrier, inc=1, device_id=to, device_id_type=pl.DeviceIdType.MESH)

    for to in partners:
        greet(to)

    @pl.when(crossed)
    def _():
        greet(swap_dev(0))

    def part(ref, i):
        return ref.at[pl.ds(pl.multiple_of(i * piece, piece), piece), :]

    def cell(zd, half, col):
        return flow_all.at[lax.rem(zd, 2), lax.div(zd, 2), half, pl.ds(pl.multiple_of(col * piece, piece), piece), :]

    def spread():
        pltpu.make_async_copy(part(flow_v, x), stage.at[0], r1.at[0]).start()
        for d in (1, 3, 2):
            send(rcopy(part(flow_v, xo(d)), stage.at[d], s1.at[d], r1.at[d], dev(x_=xo(d))))

    def roll():
        i0 = lax.broadcasted_iota(jnp.int32, (2 * LANES, LANES), 0)
        i1 = lax.broadcasted_iota(jnp.int32, (2 * LANES, LANES), 1)
        shift = jnp.where(i0 == i1 + LANES - lag, 1.0, 0.0).astype(jnp.bfloat16)
        for j in range(tiles):
            p = (j + tiles - 1) % tiles
            two = jnp.concatenate(
                [rain_v[:, p * LANES:(p + 1) * LANES], rain_v[:, j * LANES:(j + 1) * LANES]], axis=1
            )
            rain_all[z + 1, :, j * LANES:(j + 1) * LANES] = jnp.dot(
                two, shift, preferred_element_type=jnp.float32
            ).astype(jnp.bfloat16)

    def strip_of(chunk, q):
        return rain_all.at[chunk + 1, BOUNDS[q]:BOUNDS[q + 1], :]

    edges = [
        rcopy(
            rain_all.at[ZS, BOUNDS[q]:BOUNDS[q + 1], 0:LANES],
            rain_all.at[0, BOUNDS[q]:BOUNDS[q + 1], 0:LANES],
            se.at[q], re.at[q], far,
        )
        for q in range(STRIPS)
    ]

    @pl.when(yh == 0)
    def _():
        rain_all[0, :, 0:LANES] = jnp.zeros((rows, LANES), jnp.bfloat16)

    def pass_edge(chunk, q):
        pl.when((chunk == ZS - 1) & (yh == 0))(edges[q].start)

    def ring_copy(way, q, s):
        chunk = zo_(1 - s) if way == 0 else zo_(s - 1)
        at = strip_of(chunk, q)
        return rcopy(at, at, sr.at[way, q, s - 1], rr.at[way, q, s - 1], ahead if way == 0 else behind)

    def reach(way, q):
        return 4 if (q + way) % 2 == 0 else 3

    def ring_start(q):
        pass_edge(z, q)
        for way in (0, 1):
            send(ring_copy(way, q, 1))

    def ring_arrive(way, q, s):
        chunk = zo_(-s) if way == 0 else zo_(s)
        at = strip_of(chunk, q)
        rcopy(at, at, sr.at[way, q, s - 1], rr.at[way, q, s - 1], behind).wait_recv()
        if s < reach(way, q):
            send(ring_copy(way, q, s + 1))
        pass_edge(chunk, q)

    def swap(k):
        d = lax.rem(x - swap_pair(k) + XS, XS)
        src = stage.at[d]
        rcopy(src, src, s1.at[0], r1.at[d], right).wait_recv()
        dst = cell(z, yl, x)
        remote = rcopy(src, dst, s2.at[k], r2.at[k], swap_dev(k))
        if k == 0:
            send(remote, crossed)
            pl.when(jnp.logical_not(crossed))(pltpu.make_async_copy(src, dst, r2.at[0]).start)
        else:
            send(remote)

    def home(k):
        return 2 * lax.rem(zp - k + 4, 4) + c

    first = yl == other

    got = {}

    def sibling_copy(half, o):
        col = xo((0, 3, 1, 2)[o])
        at = flow_all.at[c, :, half, pl.ds(pl.multiple_of(col * piece, piece), piece), :]
        return rcopy(at, at, sc.at[half, o], rc.at[half, o], sibling)

    def to_sibling(group, half, o):
        got[group, o] = got.get((group, o), 0) + 1
        if got[group, o] == 4:
            send(sibling_copy(half, o))

    def along_x(at, j, when=None):
        send(rcopy(at, at, sx.at[0, j], rx.at[0, j], right), when)
        send(rcopy(at, at, sx.at[1, j], rx.at[1, j], left), when)

    def half_of(j):
        return other if j < 4 else yh

    def arrive_own(i):
        k = ORDER[i]
        at = cell(home(k), yl, x)
        rcopy(at, at, s2.at[k], r2.at[k], right).wait_recv()
        send(rcopy(at, at, s3.at[k], r3.at[k], near))
        along_x(at, i, first)
        to_sibling(ARRIVE_OWN, yl, 0)

    def arrive_near(i):
        k = ORDER[i]
        at = cell(home(k), 1 - yl, x)
        rcopy(at, at, s3.at[k], r3.at[k], near).wait_recv()
        along_x(at, i, jnp.logical_not(first))
        to_sibling(ARRIVE_NEAR, 1 - yl, 0)

    def late(i):
        along_x(cell(home(ORDER[i]), yh, x), i + 4)

    def arrive_x(j, o):
        at = cell(home(ORDER[j % 4]), half_of(j), xo({1: 3, 2: 1, 3: 2}[o]))
        rcopy(at, at, sx.at[o - 1, j], rx.at[o - 1, j], right).wait_recv()
        if o == 1 and j % 2 == 0:
            send(rcopy(at, at, sx.at[2, j], rx.at[2, j], right))
        if o == 2 and j % 2 == 1:
            send(rcopy(at, at, sx.at[2, j], rx.at[2, j], left))
        to_sibling(j // 4, half_of(j), o)

    def flow_ready(h):
        half = other if h == 0 else yh
        for o in range(4):
            sibling_copy(half, o).wait_recv()

    def folded(v):
        return sum(v[:, t * LANES:(t + 1) * LANES] for t in range(tiles))

    def multiply(lo, hi, h, low, high, start):
        at = slice(lo, hi)
        half = other if h == 0 else yh
        lane = lax.broadcasted_iota(jnp.int32, (hi - lo, LANES), 1)
        if start:
            acc[h, at, :] = jnp.zeros((hi - lo, rows), jnp.float32)

        def step(s, carry):
            used, cells = [], []
            for zd in (zo_(s), zo_(1 - s)):
                before = rain_all[zd, at, 0:LANES].astype(jnp.float32)
                here = rain_all[zd + 1, at, 0:LANES].astype(jnp.float32)
                head = jnp.where(lane < lag, before, here).astype(jnp.bfloat16)
                used.append(jnp.concatenate([head, rain_all[zd + 1, at, LANES:]], axis=1))
                cells.append(flow_all[lax.rem(zd, 2), lax.div(zd, 2), half])
            acc[h, at, :] += lax.dot_general(
                jnp.concatenate(used, axis=1), jnp.concatenate(cells, axis=1),
                (((1,), (1,)), ((), ())), preferred_element_type=jnp.float32,
            )
            return carry

        lax.fori_loop(low, high + 1, step, 0)

    def rain_stats(w):
        lo, hi = BOUNDS[2 * w], BOUNDS[2 * w + 2]
        lane = lax.broadcasted_iota(jnp.int32, (CUT, LANES), 1)

        def step(i, carry):
            zd = lax.rem(i, ZS)
            at = pl.ds(pl.multiple_of(lo + lax.div(i, ZS) * CUT, CUT), CUT)
            before = rain_all[zd, at, 0:LANES].astype(jnp.float32)
            wide = rain_all[zd + 1, at, :].astype(jnp.float32)
            head = jnp.where(lane < lag, before, wide[:, 0:LANES])
            wide = jnp.concatenate([head, wide[:, LANES:]], axis=1)
            rain_part[0, at, :] += folded(wide)
            rain_part[1, at, :] += folded(wide * wide)
            return carry

        lax.fori_loop(0, ZS * (hi - lo) // CUT, step, 0)

    def flow_stats(h):
        half = other if h == 0 else yh
        blocks = rows // LANES
        lanes = lax.broadcasted_iota(jnp.int32, (LANES, LANES), 1)

        def step(i, carry):
            m = lax.div(i, blocks)
            zd = 2 * m + c
            at = pl.ds(pl.multiple_of(lax.rem(i, blocks) * LANES, LANES), LANES)
            wide = flow_all[c, m, half, at, :].astype(jnp.float32)
            skip = jnp.where((yh == 0) & (zd == 0), lag, 0)
            head = jnp.where(lanes < skip, 0.0, wide[:, 0:LANES])
            wide = jnp.concatenate([head, wide[:, LANES:]], axis=1)
            flow_part[h, 0, at, :] += folded(wide)
            flow_part[h, 1, at, :] += folded(wide * wide)
            return carry

        lax.fori_loop(0, 4 * blocks, step, 0)

    def rows_of(ref, b):
        return jnp.sum(ref[b * LANES:(b + 1) * LANES, :].T, axis=0, keepdims=True)

    def share_stats():
        for b in range(rows // LANES):
            rs, rq = rows_of(rain_part.at[0], b), rows_of(rain_part.at[1], b)
            zero = jnp.zeros((4, LANES), jnp.float32)
            for i, h in ((0, 1), (1, 0)):
                fs, fq = rows_of(flow_part.at[h, 0], b), rows_of(flow_part.at[h, 1], b)
                stat_send[i, :, b * LANES:(b + 1) * LANES] = jnp.concatenate([fs, fq, rs, rq, zero], axis=0)
        for i, (src, to) in enumerate(((0, sibling), (1, far), (1, far_sibling))):
            send(rcopy(stat_send.at[src], stat_recv.at[i], st.at[i], rt.at[i], to))

    def take_stats():
        for i in range(3):
            at = stat_recv.at[i]
            rcopy(at, at, st.at[i], rt.at[i], sibling).wait_recv()
        is_flow = lax.broadcasted_iota(jnp.int32, (8, rows), 0) < 2
        halves = stat_recv[0] + stat_recv[2]
        stat_ref[...] = stat_send[0] + stat_recv[1] + jnp.where(is_flow, halves, 0.0)

    def strip_at(ref, q):
        return ref.at[BOUNDS[q]:BOUNDS[q + 1], :]

    def give(q):
        send(rcopy(strip_at(acc.at[0], q), strip_at(relay, q), sg.at[q], rg.at[q], up if q % 2 == 0 else down))

    def hand_on(q):
        at = strip_at(relay, q)
        rcopy(at, at, sg.at[q], rg.at[q], up).wait_recv()
        send(rcopy(at, strip_at(final, q), sf.at[q], rf.at[q], up if q % 2 == 0 else down))

    def finish(q):
        at = slice(BOUNDS[q], BOUNDS[q + 1])
        ref = strip_at(final, q)
        rcopy(ref, ref, sf.at[q], rf.at[q], up).wait_recv()
        cross_ref[at, :] = acc[1, at, :] + final[at, :]

    def edge_ready(wave, s):
        for zd in (zo_(s), zo_(1 - s)):

            @pl.when((zd == 0) & (yh == 1))
            def _():
                for q in wave:
                    edges[q].wait_recv()

    seen = set()

    def once(*key):
        new = key not in seen
        seen.add(key)
        return new

    def step(kind, *at):
        if kind in (MULTIPLY, FSTAT):
            h = at[1] if kind == MULTIPLY else at[0]
            if once(FSTAT, h):
                flow_ready(h)
        if kind in (MULTIPLY, RSTAT):
            w, low, high = (at[0], at[2], at[3]) if kind == MULTIPLY else (at[0], 1, 4)
            for s in range(low, high + 1):
                if once(RING, w, s):
                    edge_ready((2 * w, 2 * w + 1), s)
        if kind == MULTIPLY:
            multiply(BOUNDS[2 * w], BOUNDS[2 * w + 2], h, low, high, once(MULTIPLY, w, h))
        else:
            steps[kind](*at)

    steps = {
        SPREAD: spread, SWAP: swap, RING_START: ring_start, RING: ring_arrive,
        ARRIVE_OWN: arrive_own, ARRIVE_NEAR: arrive_near, LATE: late, ARRIVE_X: arrive_x, FSTAT: flow_stats, RSTAT: rain_stats,
        GIVE: give, HAND_ON: hand_on, SHARE: share_stats, FINISH: finish, TAKE: take_stats,
    }
    def drain():
        for copy, when in pending:
            if when is None:
                copy.wait_send()
            else:
                pl.when(when)(copy.wait_send)
        pending.clear()

    def drain_edges():
        for q in range(STRIPS):
            pl.when(yh == 0)(edges[q].wait_send)

    rain_part[...] = jnp.zeros(rain_part.shape, jnp.float32)
    flow_part[...] = jnp.zeros(flow_part.shape, jnp.float32)
    roll()
    pl.semaphore_wait(barrier, len(partners) + jnp.where(crossed, 1, 0))
    for item in SCHEDULE:
        if item[0] in (TAKE, FINISH) and once(FINISH):
            drain_edges()
            drain()
        step(*item)

    drain()


def local(rainfall, runoff, lag_days):
    rows, days = rainfall.shape
    dma = pltpu.SemaphoreType.DMA
    bf16, f32 = jnp.bfloat16, jnp.float32
    cross, stats = pl.pallas_call(
        kernel,
        out_shape=(jax.ShapeDtypeStruct((rows, rows), f32), jax.ShapeDtypeStruct((8, rows), f32)),
        in_specs=[
            pl.BlockSpec(memory_space=pltpu.SMEM),
            pl.BlockSpec(memory_space=pltpu.VMEM),
            pl.BlockSpec(memory_space=pltpu.VMEM),
        ],
        out_specs=[pl.BlockSpec(memory_space=pltpu.VMEM)] * 2,
        scratch_shapes=[
            pltpu.VMEM((XS, rows // XS, days), bf16),
            pltpu.VMEM((ZS + 1, rows, days), bf16),
            pltpu.VMEM((2, ZS // 2, 2, rows, days), bf16),
            pltpu.VMEM((2, rows, rows), f32),
            pltpu.VMEM((rows, rows), f32),
            pltpu.VMEM((rows, rows), f32),
            pltpu.VMEM((2, rows, LANES), f32),
            pltpu.VMEM((2, 2, rows, LANES), f32),
            pltpu.VMEM((2, 8, rows), f32),
            pltpu.VMEM((3, 8, rows), f32),
            dma((4,)), dma((4,)),
            dma((4,)), dma((4,)),
            dma((4,)), dma((4,)),
            dma((3, 8)), dma((3, 8)),
            dma((2, 4)), dma((2, 4)),
            dma((2, STRIPS, 4)), dma((2, STRIPS, 4)),
            dma((STRIPS,)), dma((STRIPS,)),
            dma((STRIPS,)), dma((STRIPS,)),
            dma((STRIPS,)), dma((STRIPS,)),
            dma((3,)), dma((3,)),
        ],
        compiler_params=pltpu.CompilerParams(
            collective_id=0, has_side_effects=True, vmem_limit_bytes=48 * 2**20
        ),
        cost_estimate=pl.CostEstimate(
            flops=2 * rows * 2 * rows * ZS * days, bytes_accessed=4 * rows * rows, transcendentals=0
        ),
    )(lag_days, rainfall, runoff)
    total = days * lax.axis_size("tm")
    samples = (total - lag_days[0]).astype(f32)
    flow_sum, flow_square, rain_sum, rain_square = stats[0], stats[1], stats[2], stats[3]
    covar = cross - rain_sum[:, None] * flow_sum[None, :] / samples
    rain_var = rain_square - rain_sum * rain_sum / samples
    flow_var = flow_square - flow_sum * flow_sum / samples
    return covar / jnp.sqrt(rain_var[:, None] * flow_var[None, :])


def solution(mesh):
    placed = (P("blk", "tm"), P("blk", "tm"), P())
    return jax.shard_map(
        local, mesh=mesh, in_specs=placed, out_specs=P("blk", "tm"), check_vma=False
    )
```

```python
import jax
import jax.numpy as jnp
from jax import lax
from jax.experimental import pallas as pl
from jax.experimental.pallas import tpu as pltpu
from jax.sharding import PartitionSpec as P

XS, ZS, LANES = 4, 8, 128
ORDER = (0, 1, 3, 2)
BOUNDS = (0, 176, 352, 496, 640)
STRIPS = len(BOUNDS) - 1
CUT = 32
(
    SPREAD, RING_START, SWAP, ARRIVE_OWN, RING, ARRIVE_NEAR, ARRIVE_X, LATE, MULTIPLY, GIVE, RSTAT, FSTAT, HAND_ON, SHARE, TAKE, FINISH,
) = range(16)
SCHEDULE = (
    (SPREAD,), (RING_START, 0), (RING_START, 1), (SWAP, 1), (SWAP, 0), (SWAP, 3), (ARRIVE_OWN, 0), (RING, 1, 0, 1),
    (ARRIVE_OWN, 1), (SWAP, 2), (ARRIVE_OWN, 2), (RING, 1, 0, 2), (RING, 0, 0, 1), (ARRIVE_NEAR, 0), (ARRIVE_NEAR, 1),
    (RING_START, 2), (ARRIVE_X, 0, 2), (ARRIVE_NEAR, 2), (ARRIVE_X, 0, 1), (RING, 1, 1, 1), (RING, 0, 0, 2),
    (LATE, 0), (ARRIVE_OWN, 3), (ARRIVE_X, 2, 1), (RING, 1, 1, 2), (ARRIVE_X, 1, 2), (RING, 1, 0, 3),
    (ARRIVE_X, 2, 2), (RING, 0, 1, 1), (RING, 0, 2, 1), (ARRIVE_X, 0, 3), (RING, 1, 2, 1), (RING, 0, 0, 3),
    (ARRIVE_NEAR, 3), (RING, 1, 1, 3), (ARRIVE_X, 3, 2), (LATE, 2), (RING, 1, 2, 2), (ARRIVE_X, 3, 1),
    (ARRIVE_X, 2, 3), (ARRIVE_X, 1, 1), (ARRIVE_X, 1, 3), (RING, 0, 1, 2), (RING_START, 3), (ARRIVE_X, 3, 3),
    (RING, 0, 1, 3), (RING, 0, 0, 4), (RING, 1, 2, 3), (RING, 1, 1, 4), (RING, 0, 2, 2), (ARRIVE_X, 4, 1), (LATE, 1),
    (MULTIPLY, 0, 0, 4, 4), (ARRIVE_X, 4, 2), (RING, 1, 3, 1), (LATE, 3), (MULTIPLY, 0, 0, 1, 1), (RING, 0, 3, 1),
    (MULTIPLY, 0, 0, 2, 3), (RING, 1, 3, 2), (GIVE, 1), (GIVE, 0), (ARRIVE_X, 5, 2), (MULTIPLY, 1, 0, 1, 1),
    (RING, 0, 3, 2), (ARRIVE_X, 6, 1), (ARRIVE_X, 6, 2), (RING, 0, 2, 3), (RSTAT, 0), (ARRIVE_X, 7, 2),
    (RING, 1, 3, 3), (ARRIVE_X, 4, 3), (FSTAT, 0), (ARRIVE_X, 6, 3), (RING, 0, 3, 3), (ARRIVE_X, 7, 3),
    (RING, 1, 3, 4), (ARRIVE_X, 5, 3), (HAND_ON, 0), (RING, 0, 2, 4), (HAND_ON, 1), (ARRIVE_X, 7, 1),
    (ARRIVE_X, 5, 1), (MULTIPLY, 1, 0, 2, 4), (GIVE, 2), (FSTAT, 1), (RSTAT, 1), (GIVE, 3), (SHARE,),
    (MULTIPLY, 0, 1, 1, 4), (HAND_ON, 2), (HAND_ON, 3), (MULTIPLY, 1, 1, 1, 4), (TAKE,), (FINISH, 0), (FINISH, 1),
    (FINISH, 2), (FINISH, 3),
)


def kernel(
    lag_ref, rain_v, flow_v, cross_ref, stat_ref,
    stage, rain_all, flow_all, acc, relay, final,
    rain_part, flow_part, stat_send, stat_recv,
    s1, r1, s2, r2, s3, r3, sx, rx, sc, rc, sr, rr, se, re, sg, rg, sf, rf, st, rt,
):
    rows, days = rain_v.shape
    piece = rows // XS
    assert rows == BOUNDS[-1]
    tiles = days // LANES
    lag = lag_ref[0]
    blk, tm = lax.axis_index("blk"), lax.axis_index("tm")
    yl, x, c = lax.div(blk, 8), lax.rem(lax.div(blk, 2), 4), lax.rem(blk, 2)
    yh, z = lax.div(tm, 8), lax.rem(tm, 8)
    zp, zo = lax.div(z, 2), lax.rem(z, 2)
    other = 1 - yh

    def dev(yl_=None, x_=None, c_=None, yh_=None, z_=None):
        b = (yl if yl_ is None else yl_) * 8 + (x if x_ is None else x_) * 2 + (c if c_ is None else c_)
        t = (yh if yh_ is None else yh_) * 8 + (z if z_ is None else z_)
        return (b, t)

    def xo(d):
        return lax.rem(x + d, XS)

    def zo_(d):
        return lax.rem(z + d + ZS, ZS)

    y = 2 * yh + yl
    yu, yd = lax.rem(y + 1, 4), lax.rem(y + 3, 4)
    up = dev(yl_=lax.rem(yu, 2), yh_=lax.div(yu, 2))
    down = dev(yl_=lax.rem(yd, 2), yh_=lax.div(yd, 2))
    near = dev(yl_=1 - yl)
    sibling = dev(c_=1 - c)
    far = dev(yh_=other)
    far_sibling = dev(yh_=other, c_=1 - c)
    right, left = dev(x_=xo(1)), dev(x_=xo(3))
    ahead, behind = dev(z_=zo_(1)), dev(z_=zo_(-1))

    def swap_pair(k):
        return lax.rem(zp + k, 4)

    def swap_dev(k):
        return dev(z_=2 * swap_pair(k) + c, c_=zo)

    def rcopy(src, dst, send, recv, to):
        return pltpu.make_async_remote_copy(
            src_ref=src, dst_ref=dst, send_sem=send, recv_sem=recv,
            device_id=to, device_id_type=pl.DeviceIdType.MESH,
        )

    pending = []

    def send(copy, when=None):
        if when is None:
            copy.start()
        else:
            pl.when(when)(copy.start)
        pending.append((copy, when))

    crossed = c != zo
    barrier = pltpu.get_barrier_semaphore()
    partners = [dev(x_=xo(d)) for d in (1, 2, 3)]
    partners += [ahead, behind, up, down, far, far_sibling, sibling]
    partners += [swap_dev(k) for k in (1, 2, 3)]

    def greet(to):
        pl.semaphore_signal(barrier, inc=1, device_id=to, device_id_type=pl.DeviceIdType.MESH)

    for to in partners:
        greet(to)

    @pl.when(crossed)
    def _():
        greet(swap_dev(0))

    def part(ref, i):
        return ref.at[pl.ds(pl.multiple_of(i * piece, piece), piece), :]

    def cell(zd, half, col):
        return flow_all.at[lax.rem(zd, 2), lax.div(zd, 2), half, pl.ds(pl.multiple_of(col * piece, piece), piece), :]

    def spread():
        pltpu.make_async_copy(part(flow_v, x), stage.at[0], r1.at[0]).start()
        for d in (1, 3, 2):
            send(rcopy(part(flow_v, xo(d)), stage.at[d], s1.at[d], r1.at[d], dev(x_=xo(d))))

    def roll():
        i0 = lax.broadcasted_iota(jnp.int32, (2 * LANES, LANES), 0)
        i1 = lax.broadcasted_iota(jnp.int32, (2 * LANES, LANES), 1)
        shift = jnp.where(i0 == i1 + LANES - lag, 1.0, 0.0).astype(jnp.bfloat16)
        for j in range(tiles):
            p = (j + tiles - 1) % tiles
            two = jnp.concatenate(
                [rain_v[:, p * LANES:(p + 1) * LANES], rain_v[:, j * LANES:(j + 1) * LANES]], axis=1
            )
            rain_all[z + 1, :, j * LANES:(j + 1) * LANES] = jnp.dot(
                two, shift, preferred_element_type=jnp.float32
            ).astype(jnp.bfloat16)

    def strip_of(chunk, q):
        return rain_all.at[chunk + 1, BOUNDS[q]:BOUNDS[q + 1], :]

    edges = [
        rcopy(
            rain_all.at[ZS, BOUNDS[q]:BOUNDS[q + 1], 0:LANES],
            rain_all.at[0, BOUNDS[q]:BOUNDS[q + 1], 0:LANES],
            se.at[q], re.at[q], far,
        )
        for q in range(STRIPS)
    ]

    @pl.when(yh == 0)
    def _():
        rain_all[0, :, 0:LANES] = jnp.zeros((rows, LANES), jnp.bfloat16)

    def pass_edge(chunk, q):
        pl.when((chunk == ZS - 1) & (yh == 0))(edges[q].start)

    def ring_copy(way, q, s):
        chunk = zo_(1 - s) if way == 0 else zo_(s - 1)
        at = strip_of(chunk, q)
        return rcopy(at, at, sr.at[way, q, s - 1], rr.at[way, q, s - 1], ahead if way == 0 else behind)

    def reach(way, q):
        return 4 if (q + way) % 2 == 0 else 3

    def ring_start(q):
        pass_edge(z, q)
        for way in (0, 1):
            send(ring_copy(way, q, 1))

    def ring_arrive(way, q, s):
        chunk = zo_(-s) if way == 0 else zo_(s)
        at = strip_of(chunk, q)
        rcopy(at, at, sr.at[way, q, s - 1], rr.at[way, q, s - 1], behind).wait_recv()
        if s < reach(way, q):
            send(ring_copy(way, q, s + 1))
        pass_edge(chunk, q)

    def swap(k):
        d = lax.rem(x - swap_pair(k) + XS, XS)
        src = stage.at[d]
        rcopy(src, src, s1.at[0], r1.at[d], right).wait_recv()
        dst = cell(z, yl, x)
        remote = rcopy(src, dst, s2.at[k], r2.at[k], swap_dev(k))
        if k == 0:
            send(remote, crossed)
            pl.when(jnp.logical_not(crossed))(pltpu.make_async_copy(src, dst, r2.at[0]).start)
        else:
            send(remote)

    def home(k):
        return 2 * lax.rem(zp - k + 4, 4) + c

    first = yl == other

    got = {}

    def sibling_copy(half, o):
        col = xo((0, 3, 1, 2)[o])
        at = flow_all.at[c, :, half, pl.ds(pl.multiple_of(col * piece, piece), piece), :]
        return rcopy(at, at, sc.at[half, o], rc.at[half, o], sibling)

    def to_sibling(group, half, o):
        got[group, o] = got.get((group, o), 0) + 1
        if got[group, o] == 4:
            send(sibling_copy(half, o))

    def along_x(at, j, when=None):
        send(rcopy(at, at, sx.at[0, j], rx.at[0, j], right), when)
        send(rcopy(at, at, sx.at[1, j], rx.at[1, j], left), when)

    def half_of(j):
        return other if j < 4 else yh

    def arrive_own(i):
        k = ORDER[i]
        at = cell(home(k), yl, x)
        rcopy(at, at, s2.at[k], r2.at[k], right).wait_recv()
        send(rcopy(at, at, s3.at[k], r3.at[k], near))
        along_x(at, i, first)
        to_sibling(ARRIVE_OWN, yl, 0)

    def arrive_near(i):
        k = ORDER[i]
        at = cell(home(k), 1 - yl, x)
        rcopy(at, at, s3.at[k], r3.at[k], near).wait_recv()
        along_x(at, i, jnp.logical_not(first))
        to_sibling(ARRIVE_NEAR, 1 - yl, 0)

    def late(i):
        along_x(cell(home(ORDER[i]), yh, x), i + 4)

    def arrive_x(j, o):
        at = cell(home(ORDER[j % 4]), half_of(j), xo({1: 3, 2: 1, 3: 2}[o]))
        rcopy(at, at, sx.at[o - 1, j], rx.at[o - 1, j], right).wait_recv()
        if o == 1 and j % 2 == 0:
            send(rcopy(at, at, sx.at[2, j], rx.at[2, j], right))
        if o == 2 and j % 2 == 1:
            send(rcopy(at, at, sx.at[2, j], rx.at[2, j], left))
        to_sibling(j // 4, half_of(j), o)

    def flow_ready(h):
        half = other if h == 0 else yh
        for o in range(4):
            sibling_copy(half, o).wait_recv()

    def folded(v):
        return sum(v[:, t * LANES:(t + 1) * LANES] for t in range(tiles))

    def multiply(lo, hi, h, low, high, start):
        at = slice(lo, hi)
        half = other if h == 0 else yh
        lane = lax.broadcasted_iota(jnp.int32, (hi - lo, LANES), 1)
        if start:
            acc[h, at, :] = jnp.zeros((hi - lo, rows), jnp.float32)

        def step(s, carry):
            used, cells = [], []
            for zd in (zo_(s), zo_(1 - s)):
                before = rain_all[zd, at, 0:LANES].astype(jnp.float32)
                here = rain_all[zd + 1, at, 0:LANES].astype(jnp.float32)
                head = jnp.where(lane < lag, before, here).astype(jnp.bfloat16)
                used.append(jnp.concatenate([head, rain_all[zd + 1, at, LANES:]], axis=1))
                cells.append(flow_all[lax.rem(zd, 2), lax.div(zd, 2), half])
            acc[h, at, :] += lax.dot_general(
                jnp.concatenate(used, axis=1), jnp.concatenate(cells, axis=1),
                (((1,), (1,)), ((), ())), preferred_element_type=jnp.float32,
            )
            return carry

        lax.fori_loop(low, high + 1, step, 0)

    def rain_stats(w):
        lo, hi = BOUNDS[2 * w], BOUNDS[2 * w + 2]
        lane = lax.broadcasted_iota(jnp.int32, (CUT, LANES), 1)

        def step(i, carry):
            zd = lax.rem(i, ZS)
            at = pl.ds(pl.multiple_of(lo + lax.div(i, ZS) * CUT, CUT), CUT)
            before = rain_all[zd, at, 0:LANES].astype(jnp.float32)
            wide = rain_all[zd + 1, at, :].astype(jnp.float32)
            head = jnp.where(lane < lag, before, wide[:, 0:LANES])
            wide = jnp.concatenate([head, wide[:, LANES:]], axis=1)
            rain_part[0, at, :] += folded(wide)
            rain_part[1, at, :] += folded(wide * wide)
            return carry

        lax.fori_loop(0, ZS * (hi - lo) // CUT, step, 0)

    def flow_stats(h):
        half = other if h == 0 else yh
        blocks = rows // LANES
        lanes = lax.broadcasted_iota(jnp.int32, (LANES, LANES), 1)

        def step(i, carry):
            m = lax.div(i, blocks)
            zd = 2 * m + c
            at = pl.ds(pl.multiple_of(lax.rem(i, blocks) * LANES, LANES), LANES)
            wide = flow_all[c, m, half, at, :].astype(jnp.float32)
            skip = jnp.where((yh == 0) & (zd == 0), lag, 0)
            head = jnp.where(lanes < skip, 0.0, wide[:, 0:LANES])
            wide = jnp.concatenate([head, wide[:, LANES:]], axis=1)
            flow_part[h, 0, at, :] += folded(wide)
            flow_part[h, 1, at, :] += folded(wide * wide)
            return carry

        lax.fori_loop(0, 4 * blocks, step, 0)

    def rows_of(ref, b):
        return jnp.sum(ref[b * LANES:(b + 1) * LANES, :].T, axis=0, keepdims=True)

    def share_stats():
        for b in range(rows // LANES):
            rs, rq = rows_of(rain_part.at[0], b), rows_of(rain_part.at[1], b)
            zero = jnp.zeros((4, LANES), jnp.float32)
            for i, h in ((0, 1), (1, 0)):
                fs, fq = rows_of(flow_part.at[h, 0], b), rows_of(flow_part.at[h, 1], b)
                stat_send[i, :, b * LANES:(b + 1) * LANES] = jnp.concatenate([fs, fq, rs, rq, zero], axis=0)
        for i, (src, to) in enumerate(((0, sibling), (1, far), (1, far_sibling))):
            send(rcopy(stat_send.at[src], stat_recv.at[i], st.at[i], rt.at[i], to))

    def take_stats():
        for i in range(3):
            at = stat_recv.at[i]
            rcopy(at, at, st.at[i], rt.at[i], sibling).wait_recv()
        is_flow = lax.broadcasted_iota(jnp.int32, (8, rows), 0) < 2
        halves = stat_recv[0] + stat_recv[2]
        stat_ref[...] = stat_send[0] + stat_recv[1] + jnp.where(is_flow, halves, 0.0)

    def strip_at(ref, q):
        return ref.at[BOUNDS[q]:BOUNDS[q + 1], :]

    def give(q):
        send(rcopy(strip_at(acc.at[0], q), strip_at(relay, q), sg.at[q], rg.at[q], up if q % 2 == 0 else down))

    def hand_on(q):
        at = strip_at(relay, q)
        rcopy(at, at, sg.at[q], rg.at[q], up).wait_recv()
        send(rcopy(at, strip_at(final, q), sf.at[q], rf.at[q], up if q % 2 == 0 else down))

    def finish(q):
        at = slice(BOUNDS[q], BOUNDS[q + 1])
        ref = strip_at(final, q)
        rcopy(ref, ref, sf.at[q], rf.at[q], up).wait_recv()
        cross_ref[at, :] = acc[1, at, :] + final[at, :]

    def edge_ready(wave, s):
        for zd in (zo_(s), zo_(1 - s)):

            @pl.when((zd == 0) & (yh == 1))
            def _():
                for q in wave:
                    edges[q].wait_recv()

    seen = set()

    def once(*key):
        new = key not in seen
        seen.add(key)
        return new

    def step(kind, *at):
        if kind in (MULTIPLY, FSTAT):
            h = at[1] if kind == MULTIPLY else at[0]
            if once(FSTAT, h):
                flow_ready(h)
        if kind in (MULTIPLY, RSTAT):
            w, low, high = (at[0], at[2], at[3]) if kind == MULTIPLY else (at[0], 1, 4)
            for s in range(low, high + 1):
                if once(RING, w, s):
                    edge_ready((2 * w, 2 * w + 1), s)
        if kind == MULTIPLY:
            multiply(BOUNDS[2 * w], BOUNDS[2 * w + 2], h, low, high, once(MULTIPLY, w, h))
        else:
            steps[kind](*at)

    steps = {
        SPREAD: spread, SWAP: swap, RING_START: ring_start, RING: ring_arrive,
        ARRIVE_OWN: arrive_own, ARRIVE_NEAR: arrive_near, LATE: late, ARRIVE_X: arrive_x, FSTAT: flow_stats, RSTAT: rain_stats,
        GIVE: give, HAND_ON: hand_on, SHARE: share_stats, FINISH: finish, TAKE: take_stats,
    }
    def drain():
        for copy, when in pending:
            if when is None:
                copy.wait_send()
            else:
                pl.when(when)(copy.wait_send)
        pending.clear()

    def drain_edges():
        for q in range(STRIPS):
            pl.when(yh == 0)(edges[q].wait_send)

    rain_part[...] = jnp.zeros(rain_part.shape, jnp.float32)
    flow_part[...] = jnp.zeros(flow_part.shape, jnp.float32)
    roll()
    pl.semaphore_wait(barrier, len(partners) + jnp.where(crossed, 1, 0))
    for item in SCHEDULE:
        if item[0] in (TAKE, FINISH) and once(FINISH):
            drain_edges()
            drain()
        step(*item)

    drain()


def local(rainfall, runoff, lag_days):
    rows, days = rainfall.shape
    dma = pltpu.SemaphoreType.DMA
    bf16, f32 = jnp.bfloat16, jnp.float32
    cross, stats = pl.pallas_call(
        kernel,
        out_shape=(jax.ShapeDtypeStruct((rows, rows), f32), jax.ShapeDtypeStruct((8, rows), f32)),
        in_specs=[
            pl.BlockSpec(memory_space=pltpu.SMEM),
            pl.BlockSpec(memory_space=pltpu.VMEM),
            pl.BlockSpec(memory_space=pltpu.VMEM),
        ],
        out_specs=[pl.BlockSpec(memory_space=pltpu.VMEM)] * 2,
        scratch_shapes=[
            pltpu.VMEM((XS, rows // XS, days), bf16),
            pltpu.VMEM((ZS + 1, rows, days), bf16),
            pltpu.VMEM((2, ZS // 2, 2, rows, days), bf16),
            pltpu.VMEM((2, rows, rows), f32),
            pltpu.VMEM((rows, rows), f32),
            pltpu.VMEM((rows, rows), f32),
            pltpu.VMEM((2, rows, LANES), f32),
            pltpu.VMEM((2, 2, rows, LANES), f32),
            pltpu.VMEM((2, 8, rows), f32),
            pltpu.VMEM((3, 8, rows), f32),
            dma((4,)), dma((4,)),
            dma((4,)), dma((4,)),
            dma((4,)), dma((4,)),
            dma((3, 8)), dma((3, 8)),
            dma((2, 4)), dma((2, 4)),
            dma((2, STRIPS, 4)), dma((2, STRIPS, 4)),
            dma((STRIPS,)), dma((STRIPS,)),
            dma((STRIPS,)), dma((STRIPS,)),
            dma((STRIPS,)), dma((STRIPS,)),
            dma((3,)), dma((3,)),
        ],
        compiler_params=pltpu.CompilerParams(
            collective_id=0, has_side_effects=True, vmem_limit_bytes=48 * 2**20
        ),
        cost_estimate=pl.CostEstimate(
            flops=2 * rows * 2 * rows * ZS * days, bytes_accessed=4 * rows * rows, transcendentals=0
        ),
    )(lag_days, rainfall, runoff)
    total = days * lax.axis_size("tm")
    samples = (total - lag_days[0]).astype(f32)
    flow_sum, flow_square, rain_sum, rain_square = stats[0], stats[1], stats[2], stats[3]
    covar = cross - rain_sum[:, None] * flow_sum[None, :] / samples
    rain_var = rain_square - rain_sum * rain_sum / samples
    flow_var = flow_square - flow_sum * flow_sum / samples
    return covar / jnp.sqrt(rain_var[:, None] * flow_var[None, :])


def solution(mesh):
    placed = (P("blk", "tm"), P("blk", "tm"), P())
    return jax.shard_map(
        local, mesh=mesh, in_specs=placed, out_specs=P("blk", "tm"), check_vma=False
    )
```
